256 devices in a mesh: kpt: 8 (over y_lo, x), band: 32 (over z, y_hi, core).
Axes of the slice: x: 4, y: 4 (y_hi: 2, y_lo: 2; y = y_hi * 2 + y_lo), z: 8, core: 2. Of those that a mesh axis runs over, the one named last changes fastest.
Arguments:
- targets: bfloat16 [8, 1, 2, 110592], P('kpt', None, None, 'band'), may hold values from -6 to 6
- sources: bfloat16 [8, 32, 2, 110592], P('kpt', 'band'), may hold values from -3 to 3
- kpt_coord: int32 [8, 3], replicated, may hold values from 0 to 3
Outputs:
- exchanged: float32 [8, 1, 2, 110592], P('kpt', None, None, 'band')
The draws below stay inside these ranges and needn't reach their ends.
All inputs are finite; a program needn't handle non-finite values.
Results may differ from the reference program's by a relative error of at most 0.01.
Values may be sent and summed in bfloat16 or wider, within the bound.
A program may use at most 192 MiB of HBM per device.

```python
import math
import jax
import jax.numpy as jnp
from jax import lax

NG = 48
TT = 1
NK = 8
S = 32


def place_ends(values, key, smallest, largest):
    place = [jax.random.randint(jax.random.fold_in(key, axis), (), 0, length) for axis, length in enumerate(values.shape)]
    widest = values.shape.index(max(values.shape))
    neighbour = place[:widest] + [(place[widest] + 1) % values.shape[widest]] + place[widest + 1:]
    return values.at[tuple(place)].set(smallest).at[tuple(neighbour)].set(largest)


def shard_levels(own_key, extent, shards, low, top_value):
    factor_of = 1.0
    for position, parts in shards:
        steps = jax.random.uniform(jax.random.fold_in(jax.random.fold_in(own_key, 6), position), (parts,), jnp.float32, low / len(shards), top_value / len(shards))
        factor_of = factor_of * jnp.repeat(jnp.exp(steps), extent[position] // parts).reshape((-1,) + (1,) * (len(extent) - 1 - position))
    return factor_of


def scatter_about(key, shape, scale, most, pieces=(), kind=jnp.bfloat16):
    level = shard_levels(key, shape, pieces, -0.22, 0.18) if pieces else 1.0
    values = jax.random.normal(key, shape, jnp.float32) * scale * level
    return jnp.minimum(jnp.maximum(values, -most), most).astype(kind)


def setup_inputs(seed: int = 0) -> dict:
    splits = jax.random.split(jax.random.key(seed), 4)
    return {
        "targets": scatter_about(splits[0], (NK, TT, 2, NG * NG * NG), 1.0, 6.0, ((0, 8), (3, 32))),
        "sources": scatter_about(splits[1], (NK, S, 2, NG * NG * NG), 0.5, 3.0, ((0, 8), (1, 32))),
        "kpt_coord": place_ends(jax.random.randint(splits[2], (NK, 3), 0, 4), jax.random.fold_in(splits[2], 1), 0, 3).astype(jnp.int32),
    }


def tables(grid_len):
    grid_index = jnp.arange(grid_len, dtype=jnp.int32)
    products = (grid_index[:, None] * grid_index[None, :]) % grid_len
    phases = products.astype(jnp.float32) * (2.0 * math.pi / grid_len)
    cosine = jnp.cos(phases)
    sine_part = jnp.sin(phases)
    forward = jnp.stack([jnp.stack([cosine, sine_part]), jnp.stack([-sine_part, cosine])]).astype(jnp.bfloat16)
    backward = jnp.stack([jnp.stack([cosine, -sine_part]), jnp.stack([sine_part, cosine])]).astype(jnp.bfloat16)
    return forward, backward


def kernel(q_shift, grid_len):
    grid_index = jnp.arange(grid_len, dtype=jnp.int32)
    frequency = jnp.where(grid_index < grid_len // 2, grid_index, grid_index - grid_len).astype(jnp.float32)
    sq_x = (frequency + q_shift[0]) * (frequency + q_shift[0])
    sq_y = (frequency + q_shift[1]) * (frequency + q_shift[1])
    sq_z = (frequency + q_shift[2]) * (frequency + q_shift[2])
    wave_sq = sq_x[:, None, None] + sq_y[None, :, None] + sq_z[None, None, :]
    values_out = 4.0 * math.pi / (0.04 * wave_sq + 0.25) / float(grid_len * grid_len * grid_len)
    return values_out.reshape(-1)


def transform(values_in, matrix, grid_len):
    pair_count = values_in.shape[0]
    current = values_in.reshape(pair_count, 2, grid_len, grid_len * grid_len)
    result = None
    for section_num in range(3):
        result = jnp.einsum("pqmn,tqnc->tpcm", matrix.astype(jnp.float32), current.astype(jnp.float32),
                            precision=lax.Precision.HIGHEST)
        if section_num < 2:
            current = result.astype(jnp.bfloat16).reshape(pair_count, 2, grid_len, grid_len * grid_len)
    return result.reshape(pair_count, 2, grid_len * grid_len * grid_len)


def contribution(source_block, targets_k, q_shift, forward, backward, grid_len):
    source_f = source_block.astype(jnp.float32)[:, None]
    targets_f = targets_k.astype(jnp.float32)[None]
    src_real = source_f[:, :, 0]
    src_imag = source_f[:, :, 1]
    tgt_real = targets_f[:, :, 0]
    tgt_imag = targets_f[:, :, 1]
    real_part = src_real * tgt_real + src_imag * tgt_imag
    imag_part = src_real * tgt_imag - src_imag * tgt_real
    density = jnp.stack([real_part, imag_part], axis=2).astype(jnp.bfloat16)
    band_count = density.shape[0]
    target_count = density.shape[1]
    cells = density.shape[3]
    density = density.reshape(band_count * target_count, 2, cells)
    spectrum = transform(density, forward, grid_len)
    screened = (spectrum * kernel(q_shift, grid_len)).astype(jnp.bfloat16)
    potential = transform(screened, backward, grid_len).reshape(band_count, target_count, 2, cells)
    pot_real = potential[:, :, 0]
    pot_imag = potential[:, :, 1]
    out_real = jnp.sum(src_real * pot_real - src_imag * pot_imag, axis=0)
    out_imag = jnp.sum(src_real * pot_imag + src_imag * pot_real, axis=0)
    return jnp.stack([out_real, out_imag], axis=1)


def reference(targets, sources, kpt_coord):
    forward, backward = tables(NG)
    results = []
    for target_k in range(NK):
        def step_fn(source_k, summed):
            q_shift = (kpt_coord[target_k] - kpt_coord[source_k]).astype(jnp.float32) * 0.25
            source_block = lax.dynamic_index_in_dim(sources, source_k, 0, keepdims=False)
            return summed + contribution(source_block, targets[target_k], q_shift, forward, backward, NG)
        start_sum = jnp.zeros((TT, 2, NG * NG * NG), jnp.float32)
        summed = lax.fori_loop(0, NK, step_fn, start_sum)
        results.append(summed * (-1.0 / NK))
    return jnp.stack(results)
```

```python
import functools
import math

import jax
import jax.numpy as jnp
import ml_dtypes
import numpy as np
from jax import lax
from jax.experimental import pallas as pl
from jax.experimental.pallas import tpu as pltpu
from jax.sharding import PartitionSpec as P

NG = 48
ROWS = 2 * NG
PITCH = 104
GROUP1 = 12
GROUP2 = 12
GROUP3 = 12
BF16 = jnp.bfloat16
F32 = jnp.float32
MESH = pl.DeviceIdType.MESH


def host_tables():
    index = np.arange(NG)
    phases = ((index[:, None] * index[None, :]) % NG).astype(np.float32) * np.float32(2.0 * math.pi / NG)
    half = ml_dtypes.bfloat16
    cosine = np.cos(phases).astype(half).astype(np.float32)
    sine = np.sin(phases).astype(half).astype(np.float32)
    forward = np.block([[cosine, sine], [-sine, cosine]])
    backward = np.block([[cosine, -sine], [sine, cosine]])

    def lane_table(table):
        wide = np.zeros((2, 2, 64, 2, 2, 64), np.float32)
        for p in range(2):
            for q in range(2):
                for t in range(2):
                    wide[p, t, :NG, q, t, :NG] = table[q * NG:(q + 1) * NG, p * NG:(p + 1) * NG].T
        return wide.reshape(256, 256)

    spread = np.zeros((2, 4, 256, 2, 2, 64), np.float32)
    gather = np.zeros((3, 4, 2, 64, 2, 128), np.float32)
    first_lane = [0, 0, 128, 128]
    for k in range(8):
        for z in range(NG):
            for t in range(2):
                spread[t, k // 2, 48 * k + z - first_lane[k // 2], k % 2, t, z] = 1
                for chunk in range(3):
                    lane = 48 * k + z - 128 * chunk
                    if 0 <= lane < 128:
                        gather[chunk, k - 2 * chunk, t, z, t, lane] = 1
    return [
        a.astype(half)
        for a in (
            forward,
            backward,
            lane_table(forward),
            lane_table(backward),
            spread.reshape(2, 4, 256, 256),
            gather.reshape(3, 512, 256),
        )
    ]


def dot(a, b):
    return jnp.dot(a, b, preferred_element_type=F32)


def exchange(
    kpt_ref, slice_ref, source_ref, fwd_ref, bwd_ref, zfwd_ref, zbwd_ref, spread_ref, gather_ref, out_ref,
    slots, rows_f32, dense, targ, sources, src, work1, work2, coul, total,
    sums_b, recv_c, sums_c, recv_y, sums_y, recv_z,
    gz_send, gz_recv, gy_send, gy_recv, gc_send, gc_recv, s_send, s_recv,
    rc_send, rc_recv, ry_send, ry_recv, rz_send, rz_recv,
):
    kpt = lax.axis_index("kpt")
    band = lax.axis_index("band")
    x = kpt % 4
    y = (kpt // 4) * 2 + (band // 2) % 2
    z = band // 4
    c = band % 2

    def device(x_, y_, z_, c_):
        return ((y_ // 2) * 4 + x_, z_ * 4 + (y_ % 2) * 2 + c_)

    def push(source, target, send, recv, where):
        copy = pltpu.make_async_remote_copy(
            src_ref=source, dst_ref=target, send_sem=send, recv_sem=recv, device_id=where, device_id_type=MESH
        )
        copy.start()
        return copy

    x_up = device((x + 1) % 4, y, z, c)
    x_down = device((x + 3) % 4, y, z, c)
    other = device(x, y, z, 1 - c)
    z_at = [device(x, y, (z + d) % 8, c) for d in range(8)]
    y_at = [device(x, (y + d) % 4, z, c) for d in range(4)]

    barrier = pltpu.get_barrier_semaphore()
    for peer in [x_up, x_down, other] + z_at[1:] + y_at[1:]:
        pl.semaphore_signal(barrier, inc=1, device_id=peer, device_id_type=MESH)
    pl.semaphore_wait(barrier, 13)

    to_up = push(source_ref, sources.at[1], s_send.at[0], s_recv.at[0], x_up)
    to_down = push(source_ref, sources.at[2], s_send.at[1], s_recv.at[1], x_down)

    slots[y, c, z] = slice_ref[...]
    along_z = [
        push(slots.at[y, c, z], slots.at[y, c, z], gz_send.at[d - 1], gz_recv.at[d - 1], z_at[d])
        for d in range(1, 8)
    ]
    sources[0] = source_ref[...]
    total[...] = jnp.zeros_like(total)
    for copy in along_z:
        copy.wait_recv()
    along_y = [
        push(slots.at[y, c], slots.at[y, c], gy_send.at[d - 1], gy_recv.at[d - 1], y_at[d])
        for d in range(1, 4)
    ]
    across = [push(slots.at[y, c], slots.at[y, c], gc_send.at[0], gc_recv.at[0], other)]
    for d in range(1, 4):
        along_y[d - 1].wait_recv()
        from_y = (y + 4 - d) % 4
        across.append(
            push(slots.at[from_y, c], slots.at[from_y, c], gc_send.at[d], gc_recv.at[d], other)
        )
    for copy in across:
        copy.wait_recv()

    def unpack(w, carry):
        for t in range(2):
            piece = slots[t * 2 + (w // 2) % 2, w % 2, w // 4].astype(F32)
            for p in range(2):
                rows_f32[t, pl.ds(p * 864 + 27 * w, 27), :] = piece[p * 32:p * 32 + 27]
        return carry

    lax.fori_loop(0, 32, unpack, 0)
    for t in range(2):
        for p in range(2):
            for col in range(18):
                dense[t, p * NG:(p + 1) * NG, col * 128:(col + 1) * 128] = rows_f32[
                    t, pl.ds(p * 864 + col, NG, stride=18), :
                ].astype(BF16)

    lane_from = [0, 0, 128, 256]
    table_rows = [slice(0, 128), slice(0, 256), slice(0, 256), slice(128, 256)]

    def spread_out(read, tables, store):
        for g in range(6):
            for k in range(4):
                width = 128 if k in (0, 3) else 256
                lanes = slice(384 * g + lane_from[k], 384 * g + lane_from[k] + width)
                wide = sum(
                    dot(read(i, lanes), tables(i, k, table_rows[k])) for i in range(2 if store is targ else 1)
                ).astype(BF16)
                store[8 * g + 2 * k] = wide[:, :128]
                store[8 * g + 2 * k + 1] = wide[:, 128:]

    spread_out(lambda t, lanes: dense[t, :, lanes], lambda t, k, r: spread_ref[t, k, r, :], targ)

    lane = lax.broadcasted_iota(jnp.int32, (NG, 128), 1)
    row = lax.broadcasted_iota(jnp.int32, (NG, 128), 0)
    first = lane < 64

    def frequency(i):
        return jnp.where(i < NG // 2, i, i - NG).astype(F32)

    scale = 4.0 * math.pi / float(NG**3)
    forward = fwd_ref[...]
    backward = bwd_ref[...]
    zforward = zfwd_ref[...]
    zbackward = zbwd_ref[...]

    def step(num, carry):
        @pl.when(num == 1)
        def _():
            to_up.wait_recv()
            to_down.wait_recv()
            push(sources.at[1, pl.ds(0, NG)], sources.at[3, pl.ds(0, NG)], s_send.at[2], s_recv.at[2], x_up)
            push(sources.at[2, pl.ds(NG, NG)], sources.at[3, pl.ds(NG, NG)], s_send.at[3], s_recv.at[3], x_down)

        @pl.when(num == 3)
        def _():
            for half in range(2):
                part = sources.at[3, pl.ds(half * NG, NG)]
                pltpu.make_async_remote_copy(
                    src_ref=part, dst_ref=part, send_sem=s_send.at[2 + half], recv_sem=s_recv.at[2 + half],
                    device_id=x_up if half == 0 else x_down, device_id_type=MESH,
                ).wait()

        spread_out(
            lambda i, lanes: sources[num, :, lanes],
            lambda i, k, r: spread_ref[0, k, r, :] + spread_ref[1, k, r, :],
            src,
        )
        from_k = (kpt // 4) * 4 + (x + jnp.where(num == 0, 0, jnp.where(num == 1, 3, jnp.where(num == 2, 1, 2)))) % 4

        def offset(d):
            own = kpt_ref[from_k, d]
            return jnp.where(first, kpt_ref[x, d] - own, kpt_ref[x + 4, d] - own).astype(F32) * 0.25

        fx = frequency(row) + offset(0)
        fy = frequency(row) + offset(1)
        fz = frequency(lane % 64) + offset(2)
        coul[...] = 0.04 * (fx * fx)
        fyz = 0.04 * (fy * fy + fz * fz) + 0.25

        def into_spectrum(i, carry):
            mixed = []
            for j in range(GROUP1):
                pair = []
                for cell in (2 * (i * GROUP1 + j), 2 * (i * GROUP1 + j) + 1):
                    s = src[cell].astype(F32)
                    t = targ[cell].astype(F32)
                    sr, si, tr, ti = s[:NG], s[NG:], t[:NG], t[NG:]
                    pair.append(
                        jnp.concatenate([(sr * tr + si * ti).astype(BF16), (sr * ti - si * tr).astype(BF16)], axis=0)
                    )
                after_x = dot(forward, jnp.concatenate(pair, axis=1)).astype(BF16)
                for h in (0, 128):
                    mixed.append(jnp.concatenate([after_x[:NG, h:h + 128], after_x[NG:, h:h + 128]], axis=1))
            after_z = dot(jnp.concatenate(mixed, axis=0), zforward)
            for j in range(2 * GROUP1):
                for p in range(2):
                    start = (2 * i * GROUP1 + j) * PITCH + p * NG
                    work1[pl.ds(start, NG), :] = after_z[j * NG:(j + 1) * NG, p * 128:p * 128 + 128]
            return carry

        def through_spectrum(i, carry):
            for j in range(GROUP2):
                cells = (2 * (i * GROUP2 + j), 2 * (i * GROUP2 + j) + 1)
                pair = [
                    jnp.concatenate(
                        [work1[pl.ds(cell + p * NG, NG, stride=PITCH), :].astype(BF16) for p in range(2)], axis=0
                    )
                    for cell in cells
                ]
                spectrum = dot(forward, jnp.concatenate(pair, axis=1))
                pair = []
                for h, cell in enumerate(cells):
                    factor = scale / (fyz + coul[pl.ds(cell, 1), :])
                    part = spectrum[:, h * 128:h * 128 + 128]
                    pair.append(
                        jnp.concatenate([(part[:NG] * factor).astype(BF16), (part[NG:] * factor).astype(BF16)], axis=0)
                    )
                after_y = dot(backward, jnp.concatenate(pair, axis=1))
                for h, cell in enumerate(cells):
                    work2[pl.ds(cell * PITCH, ROWS), :] = after_y[:, h * 128:h * 128 + 128]
            return carry

        def out_of_spectrum(i, carry):
            mixed = [
                jnp.concatenate(
                    [
                        work2[pl.ds(2 * i * GROUP3 + j + p * NG, NG, stride=PITCH), :].astype(BF16)
                        for p in range(2)
                    ],
                    axis=1,
                )
                for j in range(2 * GROUP3)
            ]
            after_z = dot(jnp.concatenate(mixed, axis=0), zbackward).astype(BF16)
            for j in range(GROUP3):
                pair = [
                    jnp.concatenate([after_z[n * NG:(n + 1) * NG, :128], after_z[n * NG:(n + 1) * NG, 128:]], axis=0)
                    for n in (2 * j, 2 * j + 1)
                ]
                potential = dot(backward, jnp.concatenate(pair, axis=1))
                for h in range(2):
                    cell = 2 * (i * GROUP3 + j) + h
                    s = src[cell].astype(F32)
                    sr, si = s[:NG], s[NG:]
                    pr = potential[:NG, h * 128:h * 128 + 128]
                    pi = potential[NG:, h * 128:h * 128 + 128]
                    total[cell, :NG, :] += sr * pr - si * pi
                    total[cell, NG:, :] += sr * pi + si * pr
            return carry

        lax.fori_loop(0, 24 // GROUP1, into_spectrum, 0)
        lax.fori_loop(0, 24 // GROUP2, through_spectrum, 0)
        lax.fori_loop(0, 24 // GROUP3, out_of_spectrum, 0)
        return carry

    lax.fori_loop(0, 4, step, 0)

    for g in range(6):
        for chunk in range(3):
            cells = [8 * g + 2 * chunk + k for k in range(4)]
            narrow = dot(jnp.concatenate([total[n].astype(BF16) for n in cells], axis=1), gather_ref[chunk])
            for t in range(2):
                for p in range(2):
                    rows_f32[t, pl.ds(p * 864 + 3 * g + chunk, NG, stride=18), :] = narrow[
                        p * NG:(p + 1) * NG, t * 128:t * 128 + 128
                    ]

    def pack(w, carry):
        for t in range(2):
            for p in range(2):
                sums_b[t * 2 + (w // 2) % 2, w % 2, w // 4, p * 32:p * 32 + 32, :] = rows_f32[
                    t, pl.ds(p * 864 + 27 * w, 32), :
                ].astype(BF16)
        return carry

    lax.fori_loop(0, 32, pack, 0)

    across2 = [
        push(sums_b.at[(y + d) % 4, 1 - c], recv_c.at[(y + d) % 4], rc_send.at[d], rc_recv.at[d], other)
        for d in range(4)
    ]
    along_y2 = []
    for d in (1, 2, 3, 0):
        across2[d].wait_recv()
        to_y = (y + d) % 4
        sums_c[to_y] = (sums_b[to_y, c].astype(F32) + recv_c[to_y].astype(F32)).astype(BF16)
        if d:
            along_y2.append(push(sums_c.at[to_y], recv_y.at[d - 1], ry_send.at[d - 1], ry_recv.at[d - 1], y_at[d]))
    for copy in along_y2:
        copy.wait_recv()
    sums_y[...] = sum([recv_y[d].astype(F32) for d in range(3)], sums_c[y].astype(F32)).astype(BF16)
    along_z2 = [
        push(sums_y.at[(z + d) % 8], recv_z.at[d - 1], rz_send.at[d - 1], rz_recv.at[d - 1], z_at[d])
        for d in range(1, 8)
    ]
    for copy in along_z2:
        copy.wait_recv()
    result = sum([recv_z[d].astype(F32) for d in range(7)], sums_y[z].astype(F32)) * (-1.0 / 8.0)
    out_ref[...] = result

    for copy in [to_up, to_down] + along_z + along_y + across + across2 + along_y2 + along_z2:
        copy.wait_send()


def per_device(targets, sources, kpt_coord):
    piece = jnp.pad(targets.reshape(2, 27, 128), ((0, 0), (0, 5), (0, 0))).reshape(64, 128)
    source = sources.reshape(ROWS, NG * NG)
    tables = [jnp.asarray(a) for a in host_tables()]
    vmem = pl.BlockSpec(memory_space=pltpu.VMEM)
    sems = pltpu.SemaphoreType.DMA
    out = pl.pallas_call(
        exchange,
        in_specs=[pl.BlockSpec(memory_space=pltpu.SMEM)] + [vmem] * 8,
        out_specs=vmem,
        out_shape=jax.ShapeDtypeStruct((64, 128), F32),
        scratch_shapes=[
            pltpu.VMEM((4, 2, 8, 64, 128), BF16),
            pltpu.VMEM((2, 1736, 128), F32),
            pltpu.VMEM((2, ROWS, NG * NG), BF16),
            pltpu.VMEM((NG, ROWS, 128), BF16),
            pltpu.VMEM((4, ROWS, NG * NG), BF16),
            pltpu.VMEM((NG, ROWS, 128), BF16),
            pltpu.VMEM((NG * PITCH, 128), F32),
            pltpu.VMEM((NG * PITCH, 128), F32),
            pltpu.VMEM((NG, 128), F32),
            pltpu.VMEM((NG, ROWS, 128), F32),
            pltpu.VMEM((4, 2, 8, 64, 128), BF16),
            pltpu.VMEM((4, 8, 64, 128), BF16),
            pltpu.VMEM((4, 8, 64, 128), BF16),
            pltpu.VMEM((3, 8, 64, 128), BF16),
            pltpu.VMEM((8, 64, 128), BF16),
            pltpu.VMEM((7, 64, 128), BF16),
            sems((7,)), sems((7,)), sems((3,)), sems((3,)), sems((4,)), sems((4,)), sems((4,)), sems((4,)),
            sems((4,)), sems((4,)), sems((3,)), sems((3,)), sems((7,)), sems((7,)),
        ],
        compiler_params=pltpu.CompilerParams(
            collective_id=0, has_side_effects=True, vmem_limit_bytes=48 * 2**20
        ),
    )(kpt_coord, piece, source, *tables)
    return out.reshape(2, 32, 128)[:, :27].reshape(1, 1, 2, 3456)


def solution(mesh):
    in_specs = (P("kpt", None, None, "band"), P("kpt", "band", None, None), P())
    out_specs = P("kpt", None, None, "band")
    return jax.shard_map(per_device, mesh=mesh, in_specs=in_specs, out_specs=out_specs, check_vma=False)
```

```python
import functools
import math

import jax
import jax.numpy as jnp
import ml_dtypes
import numpy as np
from jax import lax
from jax.experimental import pallas as pl
from jax.experimental.pallas import tpu as pltpu
from jax.sharding import PartitionSpec as P

NG = 48
ROWS = 2 * NG
PITCH = 104
GROUP1 = 12
GROUP2 = 12
GROUP3 = 12
SPREAD_FROM = (0, 0, 128, 256)
SPREAD_WIDE = (128, 256, 256, 128)
BF16 = jnp.bfloat16
F32 = jnp.float32
MESH = pl.DeviceIdType.MESH


def host_tables():
    index = np.arange(NG)
    phases = ((index[:, None] * index[None, :]) % NG).astype(np.float32) * np.float32(2.0 * math.pi / NG)
    half_type = ml_dtypes.bfloat16
    cosine = np.cos(phases).astype(half_type).astype(np.float32)
    sine = np.sin(phases).astype(half_type).astype(np.float32)
    forward = np.block([[cosine, sine], [-sine, cosine]])
    backward = np.block([[cosine, -sine], [sine, cosine]])

    def lane_table(table):
        wide = np.zeros((2, 2, 64, 2, 2, 64), np.float32)
        for p in range(2):
            for q in range(2):
                for t in range(2):
                    wide[p, t, :NG, q, t, :NG] = table[q * NG:(q + 1) * NG, p * NG:(p + 1) * NG].T
        return wide.reshape(256, 256)

    one = np.zeros((4, 256, 2, 2, 64), np.float32)
    two = np.zeros((4, 512, 2, 2, 64), np.float32)
    gather = np.zeros((3, 4, 2, 64, 128), np.float32)
    for k in range(8):
        lanes = slice(48 * k - SPREAD_FROM[k // 2], 48 * (k + 1) - SPREAD_FROM[k // 2])
        width = SPREAD_WIDE[k // 2]
        for half in range(2):
            one[k // 2, lanes, k % 2, half, :NG] = np.eye(NG)
            two[k // 2, lanes.start + half * width:lanes.stop + half * width, k % 2, half, :NG] = np.eye(NG)
            for chunk in range(3):
                for z in range(NG):
                    lane = 48 * k + z - 128 * chunk
                    if 0 <= lane < 128:
                        gather[chunk, k - 2 * chunk, half, z, lane] = 1
    return [
        a.astype(half_type)
        for a in (
            forward,
            backward,
            lane_table(forward),
            lane_table(backward),
            one.reshape(4, 256, 256),
            two.reshape(4, 512, 256),
            gather.reshape(3, 512, 128),
        )
    ]


def dot(a, b):
    return jnp.dot(a, b, preferred_element_type=F32)


def exchange(
    kpt_hbm, slice_ref, source_ref, fwd_hbm, bwd_hbm, zfwd_hbm, zbwd_hbm, one_hbm, two_hbm, gather_hbm, out_ref,
    kpt_ref, fwd_ref, bwd_ref, zfwd_ref, zbwd_ref, one_ref, two_ref, gather_ref,
    staged, piece, slots, rows_f32, dense, targ, sources, src, work1, work2, coul, total,
    chunk_f32, chunks, passing, arrived, sums, parts, finals,
    in_sem, gz_send, gz_recv, gy_send, gy_recv, s_send, s_recv, c_send, c_recv,
    rm_send, rm_recv, ry_send, ry_recv, rz_send, rz_recv,
):
    kpt = lax.axis_index("kpt")
    band = lax.axis_index("band")
    x = kpt % 4
    y = (kpt // 4) + ((band // 2) % 2) * 2
    z = band // 4
    c = band % 2
    mine = y // 2
    primary = c == y % 2

    def device(x_, y_, z_, c_):
        return ((y_ % 2) * 4 + x_, z_ * 4 + (y_ // 2) * 2 + c_)

    def link(source, target, send, recv, where):
        return pltpu.make_async_remote_copy(
            src_ref=source, dst_ref=target, send_sem=send, recv_sem=recv, device_id=where, device_id_type=MESH
        )

    def push(*args):
        copy = link(*args)
        copy.start()
        return copy

    x_up = device((x + 1) % 4, y, z, c)
    x_down = device((x + 3) % 4, y, z, c)
    y_up = device(x, (y + 1) % 4, z, c)
    y_down = device(x, (y + 3) % 4, z, c)
    other = device(x, y, z, 1 - c)

    fetched = [
        pltpu.make_async_copy(a, b, in_sem.at[i])
        for i, (a, b) in enumerate(
            (
                (kpt_hbm, kpt_ref), (fwd_hbm, fwd_ref), (bwd_hbm, bwd_ref), (zfwd_hbm, zfwd_ref),
                (zbwd_hbm, zbwd_ref), (one_hbm, one_ref), (two_hbm, two_ref), (gather_hbm, gather_ref),
            )
        )
    ]
    for copy in fetched:
        copy.start()

    barrier = pltpu.get_barrier_semaphore()
    peers = [device(x, y, (z + d) % 8, e) for d in range(1, 8) for e in range(2)]
    for peer in [x_up, x_down, y_up, y_down, other] + peers:
        pl.semaphore_signal(barrier, inc=1, device_id=peer, device_id_type=MESH)

    for k in range(27):
        pair = slice_ref[:, 128 * k:128 * k + 128].astype(F32)
        staged[k:k + 1, :] = pair[0:1]
        staged[32 + k:33 + k, :] = pair[1:2]
    piece[...] = staged[...].astype(BF16)

    pl.semaphore_wait(barrier, 19)

    def to_primary(d):
        return link(
            piece, slots.at[mine, z, c], gz_send.at[d], gz_recv.at[d, c], device(x, y, (z + d) % 8, y % 2)
        )

    for d in range(1, 8):
        to_primary(d).start()

    @pl.when(jnp.logical_not(primary))
    def _():
        to_primary(0).start()

    low = pl.ds(0, NG)
    high = pl.ds(NG, NG)
    up_sends = [
        push(source_ref.at[part], sources.at[1, c, part], s_send.at[n], s_recv.at[n], x_up)
        for n, part in ((0, low), (2, high))
    ]
    down_sends = [
        push(source_ref.at[part], sources.at[2, c, part], s_send.at[n], s_recv.at[n], x_down)
        for n, part in ((1, high), (3, low))
    ]
    beside = push(source_ref, sources.at[0, c], c_send.at[0], c_recv.at[0], other)
    sources[0, c] = source_ref[...]

    @pl.when(primary)
    def _():
        slots[mine, z, c] = piece[...]

    total[...] = jnp.zeros_like(total)

    def across(num):
        return link(sources.at[num, c], sources.at[num, c], c_send.at[num], c_recv.at[num], other)

    def relay(n):
        part, frm, to = ((low, 1, x_up), (high, 2, x_down))[n]
        return link(
            sources.at[frm, c, part], sources.at[3, c, part], s_send.at[4 + n], s_recv.at[4 + n], to
        )

    first = pl.ds(0, 4)
    second = pl.ds(4, 4)

    def along_y(n, who, to):
        part = (first, second, second, first)[n]
        return link(slots.at[who, part], slots.at[who, part], gy_send.at[n], gy_recv.at[n], to)

    @pl.when(primary)
    def _():
        for d in range(8):
            for e in range(2):
                if d:
                    link(
                        piece, slots.at[mine, z, c], gz_send.at[d], gz_recv.at[d, e], other
                    ).wait_recv()
        link(piece, slots.at[mine, z, c], gz_send.at[0], gz_recv.at[0, 1 - c], other).wait_recv()
        for n, to in ((0, y_up), (1, y_down), (2, y_up), (3, y_down)):
            along_y(n, mine, to).start()

    up_sends[0].wait_recv()
    relay(0).start()
    down_sends[0].wait_recv()
    relay(1).start()

    @pl.when(primary)
    def _():
        along_y(0, 1 - mine, y_up).wait_recv()
        along_y(1, 1 - mine, y_down).wait_recv()
        for n, to in ((0, y_up), (1, y_down), (2, y_up), (3, y_down)):
            along_y(n, mine, to).wait_send()

    below = ((y + 3) % 4) // 2
    above = ((y + 1) % 4) // 2

    @pl.when(jnp.logical_not(primary))
    def _():
        along_y(0, below, y_up).wait_recv()
        along_y(0, below, y_up).start()
        along_y(1, above, y_down).wait_recv()
        along_y(1, above, y_down).start()
        along_y(2, below, y_up).wait_recv()
        along_y(3, above, y_down).wait_recv()
        along_y(0, below, y_up).wait_send()
        along_y(1, above, y_down).wait_send()

    def unpack(z_, carry):
        for h in range(2):
            for e in range(2):
                got = slots[h, z_, e].astype(F32)
                for p in range(2):
                    rows_f32[pl.ds(p * 864 + 108 * z_ + 54 * h + 27 * e, 27), :] = got[p * 32:p * 32 + 27]
        return carry

    lax.fori_loop(0, 8, unpack, 0)
    for p in range(2):
        for col in range(18):
            dense[p * NG:(p + 1) * NG, col * 128:(col + 1) * 128] = rows_f32[
                pl.ds(p * 864 + col, NG, stride=18), :
            ].astype(BF16)

    for copy in fetched:
        copy.wait()

    def spread_out(read, table, copies, store):
        for g in range(6):
            for k in range(4):
                width = SPREAD_WIDE[k]
                lanes = slice(384 * g + SPREAD_FROM[k], 384 * g + SPREAD_FROM[k] + width)
                rows = [read(i, lanes) for i in range(copies)]
                wide = dot(rows[0] if copies == 1 else jnp.concatenate(rows, axis=1), table[k, :copies * width, :])
                wide = wide.astype(BF16)
                store[8 * g + 2 * k] = wide[:, :128]
                store[8 * g + 2 * k + 1] = wide[:, 128:]

    spread_out(lambda i, lanes: dense[:, lanes], one_ref, 1, targ)

    up_sends[1].wait_recv()
    across(1).start()

    lane = lax.broadcasted_iota(jnp.int32, (NG, 128), 1)
    row = lax.broadcasted_iota(jnp.int32, (NG, 128), 0)

    def frequency(i):
        return jnp.where(i < NG // 2, i, i - NG).astype(F32)

    scale = 4.0 * math.pi / float(NG**3)
    forward = fwd_ref[...]
    backward = bwd_ref[...]
    zforward = zfwd_ref[...]
    zbackward = zbwd_ref[...]

    def step(num, carry):
        @pl.when(num == 1)
        def _():
            down_sends[1].wait_recv()
            across(2).start()

        @pl.when(num == 2)
        def _():
            relay(0).wait_recv()
            relay(1).wait_recv()
            across(3).start()

        across(num).wait_recv()
        spread_out(lambda i, lanes: sources[num, i, :, lanes], two_ref, 2, src)
        from_x = jnp.where(num == 0, 0, jnp.where(num == 1, 3, jnp.where(num == 2, 1, 2)))
        from_k = (kpt // 4) * 4 + (x + from_x) % 4

        def offset(d):
            return (kpt_ref[c * 4 + x, d] - kpt_ref[from_k, d]).astype(F32) * 0.25

        fx = frequency(row) + offset(0)
        fy = frequency(row) + offset(1)
        fz = frequency(lane % 64) + offset(2)
        coul[...] = 0.04 * (fx * fx)
        fyz = 0.04 * (fy * fy + fz * fz) + 0.25

        def into_spectrum(i, carry):
            mixed = []
            for j in range(GROUP1):
                pair = []
                for cell in (2 * (i * GROUP1 + j), 2 * (i * GROUP1 + j) + 1):
                    s = src[cell].astype(F32)
                    t = targ[cell].astype(F32)
                    sr, si, tr, ti = s[:NG], s[NG:], t[:NG], t[NG:]
                    pair.append(
                        jnp.concatenate([(sr * tr + si * ti).astype(BF16), (sr * ti - si * tr).astype(BF16)], axis=0)
                    )
                after_x = dot(forward, jnp.concatenate(pair, axis=1)).astype(BF16)
                for h in (0, 128):
                    mixed.append(jnp.concatenate([after_x[:NG, h:h + 128], after_x[NG:, h:h + 128]], axis=1))
            after_z = dot(jnp.concatenate(mixed, axis=0), zforward)
            for j in range(2 * GROUP1):
                for p in range(2):
                    start = (2 * i * GROUP1 + j) * PITCH + p * NG
                    work1[pl.ds(start, NG), :] = after_z[j * NG:(j + 1) * NG, p * 128:p * 128 + 128]
            return carry

        def through_spectrum(i, carry):
            for j in range(GROUP2):
                cells = (2 * (i * GROUP2 + j), 2 * (i * GROUP2 + j) + 1)
                pair = [
                    jnp.concatenate(
                        [work1[pl.ds(cell + p * NG, NG, stride=PITCH), :].astype(BF16) for p in range(2)], axis=0
                    )
                    for cell in cells
                ]
                spectrum = dot(forward, jnp.concatenate(pair, axis=1))
                pair = []
                for h, cell in enumerate(cells):
                    factor = scale / (fyz + coul[pl.ds(cell, 1), :])
                    part = spectrum[:, h * 128:h * 128 + 128]
                    pair.append(
                        jnp.concatenate([(part[:NG] * factor).astype(BF16), (part[NG:] * factor).astype(BF16)], axis=0)
                    )
                after_y = dot(backward, jnp.concatenate(pair, axis=1))
                for h, cell in enumerate(cells):
                    work2[pl.ds(cell * PITCH, ROWS), :] = after_y[:, h * 128:h * 128 + 128]
            return carry

        def out_of_spectrum(i, carry):
            mixed = [
                jnp.concatenate(
                    [
                        work2[pl.ds(2 * i * GROUP3 + j + p * NG, NG, stride=PITCH), :].astype(BF16)
                        for p in range(2)
                    ],
                    axis=1,
                )
                for j in range(2 * GROUP3)
            ]
            after_z = dot(jnp.concatenate(mixed, axis=0), zbackward).astype(BF16)
            for j in range(GROUP3):
                pair = [
                    jnp.concatenate([after_z[n * NG:(n + 1) * NG, :128], after_z[n * NG:(n + 1) * NG, 128:]], axis=0)
                    for n in (2 * j, 2 * j + 1)
                ]
                potential = dot(backward, jnp.concatenate(pair, axis=1))
                for h in range(2):
                    cell = 2 * (i * GROUP3 + j) + h
                    s = src[cell].astype(F32)
                    sr, si = s[:NG], s[NG:]
                    pr = potential[:NG, h * 128:h * 128 + 128]
                    pi = potential[NG:, h * 128:h * 128 + 128]
                    total[cell, :NG, :] += sr * pr - si * pi
                    total[cell, NG:, :] += sr * pi + si * pr
            return carry

        lax.fori_loop(0, 24 // GROUP1, into_spectrum, 0)
        lax.fori_loop(0, 24 // GROUP2, through_spectrum, 0)
        lax.fori_loop(0, 24 // GROUP3, out_of_spectrum, 0)
        return carry

    lax.fori_loop(0, 4, step, 0)

    for g in range(6):
        for chunk in range(3):
            cells = [8 * g + 2 * chunk + k for k in range(4)]
            narrow = dot(jnp.concatenate([total[n].astype(BF16) for n in cells], axis=1), gather_ref[chunk])
            for p in range(2):
                rows_f32[pl.ds(p * 864 + 3 * g + chunk, NG, stride=18), :] = narrow[p * NG:(p + 1) * NG]

    def pack(z_, carry):
        for h in range(2):
            for p in range(2):
                chunk_f32[h, p, pl.ds(54 * z_, 54), :] = rows_f32[pl.ds(p * 864 + 108 * z_ + 54 * h, 54), :]
        return carry

    lax.fori_loop(0, 8, pack, 0)
    chunks[...] = chunk_f32[:, :, :432, :].astype(BF16)

    def middle(n):
        return link(
            chunks.at[1 - mine, n], passing.at[n], rm_send.at[n], rm_recv.at[n], (y_down, y_up)[n]
        )

    def onward(n, p, buffer):
        return link(buffer, arrived.at[n, p], ry_send.at[n, p], ry_recv.at[n, p], (y_up, y_down)[n])

    @pl.when(primary)
    def _():
        middle(0).start()
        middle(1).start()

    @pl.when(jnp.logical_not(primary))
    def _():
        onward(0, 0, chunks.at[above, 0]).start()
        onward(1, 1, chunks.at[below, 1]).start()
        middle(0).wait_recv()
        chunks[below, 0] = (chunks[below, 0].astype(F32) + passing[0].astype(F32)).astype(BF16)
        onward(1, 0, chunks.at[below, 0]).start()
        middle(1).wait_recv()
        chunks[above, 1] = (chunks[above, 1].astype(F32) + passing[1].astype(F32)).astype(BF16)
        onward(0, 1, chunks.at[above, 1]).start()

    def share(d, e):
        return link(
            parts.at[(z + d) % 8, e], finals.at[d], rz_send.at[d, e], rz_recv.at[d], device(x, y, (z + d) % 8, e)
        )

    @pl.when(primary)
    def _():
        for p in range(2):
            onward(0, p, chunks.at[0, p]).wait_recv()
            onward(1, p, chunks.at[0, p]).wait_recv()
            sums[p, :432, :] = (
                chunks[mine, p].astype(F32) + arrived[0, p].astype(F32) + arrived[1, p].astype(F32)
            )

        def split(z_, carry):
            for e in range(2):
                for p in range(2):
                    parts[z_, e, p * 32:p * 32 + 32, :] = sums[p, pl.ds(54 * z_ + 27 * e, 32), :].astype(BF16)
            return carry

        lax.fori_loop(0, 8, split, 0)
        for d in range(1, 8):
            for e in range(2):
                share(d, e).start()
        share(0, 1 - c).start()
        finals[0] = parts[z, c]

    @pl.when(jnp.logical_not(primary))
    def _():
        share(0, c).wait_recv()

    for d in range(1, 8):
        share(d, c).wait_recv()
    result = sum([finals[d].astype(F32) for d in range(1, 8)], finals[0].astype(F32)) * (-1.0 / 8.0)
    for k in range(27):
        for p in range(2):
            out_ref[p:p + 1, 128 * k:128 * k + 128] = result[p * 32 + k:p * 32 + k + 1]

    for d in range(1, 8):
        to_primary(d).wait_send()
    for copy in up_sends + down_sends + [across(n) for n in range(4)] + [relay(0), relay(1)]:
        copy.wait_send()

    @pl.when(primary)
    def _():
        for n in range(2):
            middle(n).wait_send()
        for d in range(1, 8):
            for e in range(2):
                share(d, e).wait_send()
        share(0, 1 - c).wait_send()

    @pl.when(jnp.logical_not(primary))
    def _():
        to_primary(0).wait_send()
        for n in range(2):
            for p in range(2):
                onward(n, p, chunks.at[0, p]).wait_send()


def per_device(targets, sources, kpt_coord):
    tables = [jnp.asarray(a) for a in host_tables()]
    vmem = pl.BlockSpec(memory_space=pltpu.VMEM)
    anywhere = pl.BlockSpec(memory_space=pl.ANY)
    sems = pltpu.SemaphoreType.DMA
    out = pl.pallas_call(
        exchange,
        in_specs=[anywhere, vmem, vmem] + [anywhere] * 7,
        out_specs=vmem,
        out_shape=jax.ShapeDtypeStruct((2, 3456), F32),
        scratch_shapes=[pltpu.SMEM((8, 3), jnp.int32)]
        + [pltpu.VMEM(a.shape, BF16) for a in tables]
        + [
            pltpu.VMEM((64, 128), F32),
            pltpu.VMEM((64, 128), BF16),
            pltpu.VMEM((2, 8, 2, 64, 128), BF16),
            pltpu.VMEM((1736, 128), F32),
            pltpu.VMEM((ROWS, NG * NG), BF16),
            pltpu.VMEM((NG, ROWS, 128), BF16),
            pltpu.VMEM((4, 2, ROWS, NG * NG), BF16),
            pltpu.VMEM((NG, ROWS, 128), BF16),
            pltpu.VMEM((NG * PITCH, 128), F32),
            pltpu.VMEM((NG * PITCH, 128), F32),
            pltpu.VMEM((NG, 128), F32),
            pltpu.VMEM((NG, ROWS, 128), F32),
            pltpu.VMEM((2, 2, 440, 128), F32),
            pltpu.VMEM((2, 2, 432, 128), BF16),
            pltpu.VMEM((2, 432, 128), BF16),
            pltpu.VMEM((2, 2, 432, 128), BF16),
            pltpu.VMEM((2, 440, 128), F32),
            pltpu.VMEM((8, 2, 64, 128), BF16),
            pltpu.VMEM((8, 64, 128), BF16),
            sems((8,)), sems((8,)), sems((8, 2)), sems((4,)), sems((4,)), sems((6,)), sems((6,)),
            sems((4,)), sems((4,)), sems((2,)), sems((2,)), sems((2, 2)), sems((2, 2)), sems((8, 2)), sems((8,)),
        ],
        compiler_params=pltpu.CompilerParams(
            collective_id=0, has_side_effects=True, vmem_limit_bytes=48 * 2**20
        ),
    )(kpt_coord, targets.reshape(2, 3456), sources.reshape(ROWS, NG * NG), *tables)
    return out.reshape(1, 1, 2, 3456)


def solution(mesh):
    in_specs = (P("kpt", None, None, "band"), P("kpt", "band", None, None), P())
    out_specs = P("kpt", None, None, "band")
    return jax.shard_map(per_device, mesh=mesh, in_specs=in_specs, out_specs=out_specs, check_vma=False)
```

```python
import functools
import math

import jax
import jax.numpy as jnp
import ml_dtypes
import numpy as np
from jax import lax
from jax.experimental import pallas as pl
from jax.experimental.pallas import tpu as pltpu
from jax.sharding import PartitionSpec as P

NG = 48
ROWS = 2 * NG
PITCH = 104
GROUP1 = 24
GROUP2 = 24
GROUP3 = 24
BATCH = 2
SPAN = NG * PITCH
SPREAD_FROM = (0, 0, 128, 256)
SPREAD_WIDE = (128, 256, 256, 128)
BF16 = jnp.bfloat16
F32 = jnp.float32
MESH = pl.DeviceIdType.MESH


def host_tables():
    index = np.arange(NG)
    phases = ((index[:, None] * index[None, :]) % NG).astype(np.float32) * np.float32(2.0 * math.pi / NG)
    half_type = ml_dtypes.bfloat16
    cosine = np.cos(phases).astype(half_type).astype(np.float32)
    sine = np.sin(phases).astype(half_type).astype(np.float32)
    forward = np.block([[cosine, sine], [-sine, cosine]])
    backward = np.block([[cosine, -sine], [sine, cosine]])

    def lane_table(table):
        wide = np.zeros((2, 2, 64, 2, 2, 64), np.float32)
        for p in range(2):
            for q in range(2):
                for t in range(2):
                    wide[p, t, :NG, q, t, :NG] = table[q * NG:(q + 1) * NG, p * NG:(p + 1) * NG].T
        return wide.reshape(256, 256)

    one = np.zeros((4, 256, 2, 2, 64), np.float32)
    two = np.zeros((4, 512, 2, 2, 64), np.float32)
    gather = np.zeros((3, 4, 2, 64, 128), np.float32)
    for k in range(8):
        lanes = slice(48 * k - SPREAD_FROM[k // 2], 48 * (k + 1) - SPREAD_FROM[k // 2])
        width = SPREAD_WIDE[k // 2]
        for half in range(2):
            one[k // 2, lanes, k % 2, half, :NG] = np.eye(NG)
            two[k // 2, lanes.start + half * width:lanes.stop + half * width, k % 2, half, :NG] = np.eye(NG)
            for chunk in range(3):
                for z in range(NG):
                    lane = 48 * k + z - 128 * chunk
                    if 0 <= lane < 128:
                        gather[chunk, k - 2 * chunk, half, z, lane] = 1
    return [
        a.astype(half_type)
        for a in (
            forward,
            backward,
            lane_table(forward),
            lane_table(backward),
            one.reshape(4, 256, 256),
            two.reshape(4, 512, 256),
            gather.reshape(3, 512, 128),
        )
    ]


def dot(a, b):
    return jnp.dot(a, b, preferred_element_type=F32)


def exchange(
    kpt_hbm, slice_hbm, source_hbm, fwd_hbm, bwd_hbm, zfwd_hbm, zbwd_hbm, one_hbm, two_hbm, gather_hbm, out_ref,
    kpt_ref, slice_ref, raw_ref, fwd_ref, bwd_ref, zfwd_ref, zbwd_ref, one_ref, two_ref, gather_ref,
    staged, piece, carried, slots, rows_f32, dense, targ, sources, src, work1, work2, coul, base, total,
    chunks, arrived, parts, finals,
    in_sem, gz_send, gz_recv, gy_send, gy_recv, s_send, s_recv, c_send, c_recv,
    ry_send, ry_recv, rz_send, rz_recv,
):
    kpt = lax.axis_index("kpt")
    band = lax.axis_index("band")
    x = kpt % 4
    y = (kpt // 4) + ((band // 2) % 2) * 2
    z = band // 4
    c = band % 2
    mine = y // 2
    primary = c == y % 2
    secondary = c != y % 2

    def device(x_, y_, z_, c_):
        return ((y_ % 2) * 4 + x_, z_ * 4 + (y_ // 2) * 2 + c_)

    def link(source, target, send, recv, where):
        return pltpu.make_async_remote_copy(
            src_ref=source, dst_ref=target, send_sem=send, recv_sem=recv, device_id=where, device_id_type=MESH
        )

    x_up = device((x + 1) % 4, y, z, c)
    x_down = device((x + 3) % 4, y, z, c)
    other = device(x, y, z, 1 - c)

    fetched = [
        pltpu.make_async_copy(a, b, in_sem.at[i])
        for i, (a, b) in enumerate(
            (
                (slice_hbm, slice_ref), (source_hbm, raw_ref), (kpt_hbm, kpt_ref), (one_hbm, one_ref),
                (two_hbm, two_ref), (fwd_hbm, fwd_ref), (bwd_hbm, bwd_ref), (zfwd_hbm, zfwd_ref),
                (zbwd_hbm, zbwd_ref), (gather_hbm, gather_ref),
            )
        )
    ]
    for copy in fetched:
        copy.start()

    barrier = pltpu.get_barrier_semaphore()
    peers = [x_up, x_down, other] + [device(x, y, (z + d) % 8, c) for d in range(1, 8)]
    peers += [device(x, (y + d) % 4, z, e) for d in range(1, 4) for e in range(2)]
    for peer in peers:
        pl.semaphore_signal(barrier, inc=1, device_id=peer, device_id_type=MESH)

    fetched[0].wait()
    for k in range(27):
        staged[2 * k:2 * k + 2, :] = slice_ref[:, 128 * k:128 * k + 128].astype(F32)
    piece[...] = staged[...].astype(BF16)

    pl.semaphore_wait(barrier, len(peers))

    def along_z(d):
        return link(piece, carried.at[z], gz_send.at[d], gz_recv.at[d], device(x, y, (z + d) % 8, c))

    def along_y(d, held, z_):
        return link(
            held, slots.at[mine, c, z_], gy_send.at[d], gy_recv.at[d, c], device(x, (y + d) % 4, z, y % 2)
        )

    def spread_y(held, z_):
        for d in range(1, 4):
            along_y(d, held, z_).start()

        @pl.when(secondary)
        def _():
            along_y(0, held, z_).start()

    for d in (4, 3, 5, 2, 6, 1, 7):
        along_z(d).start()
    spread_y(piece, z)

    fetched[1].wait()

    def densify(raw, store):
        for p in range(2):
            for col in range(18):
                store(p, col, raw[pl.ds(2 * col + p, NG, stride=36), :].astype(BF16))

    rows_f32[pl.ds(0, 2 * 864), :] = raw_ref[...].astype(F32)

    def keep_source(p, col, block):
        sources[0, c, p * NG:(p + 1) * NG, col * 128:(col + 1) * 128] = block

    densify(rows_f32, keep_source)

    low = pl.ds(0, NG)
    high = pl.ds(NG, NG)
    legs = ((low, 1, x_up), (high, 2, x_down), (high, 1, x_up), (low, 2, x_down))

    def along_x(n):
        part, place, to = legs[n]
        return link(sources.at[0, c, part], sources.at[place, c, part], s_send.at[n], s_recv.at[n], to)

    def relay(n):
        part, place, to = legs[n]
        return link(sources.at[place, c, part], sources.at[3, c, part], s_send.at[4 + n], s_recv.at[4 + n], to)

    def across(num):
        return link(sources.at[num, c], sources.at[num, c], c_send.at[num], c_recv.at[num], other)

    for n in range(4):
        along_x(n).start()
    across(0).start()
    total[...] = jnp.zeros_like(total)

    for d in (1, 7, 2, 6, 3, 5, 4):
        along_z(d).wait_recv()
        from_z = (z + 8 - d) % 8
        spread_y(carried.at[from_z], from_z)

    along_x(0).wait_recv()
    relay(0).start()
    along_x(1).wait_recv()
    relay(1).start()

    def group(d, h, e):
        whole = slots.at[h, e]
        return link(whole, whole, gy_send.at[d], gy_recv.at[d, e], other)

    @pl.when(primary)
    def _():
        carried[z] = piece[...]
        slots[mine, c] = carried[...]
        group(0, mine, 1 - c).wait_recv()
        for e in range(2):
            group(2, 1 - mine, e).wait_recv()

    @pl.when(secondary)
    def _():
        for e in range(2):
            group(1, ((y + 3) % 4) // 2, e).wait_recv()
            group(3, ((y + 1) % 4) // 2, e).wait_recv()

    def unpack(z_, carry):
        for h in range(2):
            for e in range(2):
                start = 54 * (4 * z_ + 2 * h + e)
                rows_f32[pl.ds(start, 54), :] = slots[h, e, z_].astype(F32)[:54]
        return carry

    lax.fori_loop(0, 8, unpack, 0)

    def keep_target(p, col, block):
        dense[p * NG:(p + 1) * NG, col * 128:(col + 1) * 128] = block

    densify(rows_f32, keep_target)

    for copy in fetched[2:]:
        copy.wait()

    def spread_out(read, table, copies, store):
        for g in range(6):
            for k in range(4):
                width = SPREAD_WIDE[k]
                lanes = slice(384 * g + SPREAD_FROM[k], 384 * g + SPREAD_FROM[k] + width)
                rows = [read(i, lanes) for i in range(copies)]
                wide = dot(rows[0] if copies == 1 else jnp.concatenate(rows, axis=1), table[k, :copies * width, :])
                wide = wide.astype(BF16)
                store(8 * g + 2 * k, wide[:, :128])
                store(8 * g + 2 * k + 1, wide[:, 128:])

    def set_target(cell, block):
        targ[cell] = block

    spread_out(lambda i, lanes: dense[:, lanes], one_ref, 1, set_target)

    along_x(2).wait_recv()
    across(1).start()

    lane = lax.broadcasted_iota(jnp.int32, (NG, 128), 1)
    row = lax.broadcasted_iota(jnp.int32, (NG, 128), 0)

    def frequency(i):
        return jnp.where(i < NG // 2, i, i - NG).astype(F32)

    scale = 4.0 * math.pi / float(NG**3)
    forward = fwd_ref[...]
    backward = bwd_ref[...]
    zforward = zfwd_ref[...]
    zbackward = zbwd_ref[...]

    def prepare(num, carry):
        @pl.when(num == 2)
        def _():
            along_x(3).wait_recv()
            across(2).start()
            relay(0).wait_recv()
            relay(1).wait_recv()
            across(3).start()

        across(num).wait_recv()
        at = num % BATCH

        def set_source(cell, block):
            src[at, cell] = block

        spread_out(lambda i, lanes: sources[num, i, :, lanes], two_ref, 2, set_source)
        from_x = jnp.where(num == 0, 0, jnp.where(num == 1, 3, jnp.where(num == 2, 1, 2)))
        from_k = (kpt // 4) * 4 + (x + from_x) % 4

        def offset(d):
            return (kpt_ref[d, c * 4 + x] - kpt_ref[d, from_k]).astype(F32) * 0.25

        fx = frequency(row) + offset(0)
        fy = frequency(row) + offset(1)
        fz = frequency(lane % 64) + offset(2)
        coul[at] = 0.04 * (fx * fx)
        base[at] = 0.04 * (fy * fy + fz * fz) + 0.25
        return carry

    def into_spectrum(at, i):
        mixed = []
        for j in range(GROUP1):
            pair = []
            for cell in (2 * (i * GROUP1 + j), 2 * (i * GROUP1 + j) + 1):
                s = src[at, cell].astype(F32)
                t = targ[cell].astype(F32)
                sr, si, tr, ti = s[:NG], s[NG:], t[:NG], t[NG:]
                pair.append(
                    jnp.concatenate([(sr * tr + si * ti).astype(BF16), (sr * ti - si * tr).astype(BF16)], axis=0)
                )
            after_x = dot(forward, jnp.concatenate(pair, axis=1)).astype(BF16)
            for h in (0, 128):
                mixed.append(jnp.concatenate([after_x[:NG, h:h + 128], after_x[NG:, h:h + 128]], axis=1))
        after_z = dot(jnp.concatenate(mixed, axis=0), zforward)
        for j in range(2 * GROUP1):
            for p in range(2):
                start = at * SPAN + (2 * i * GROUP1 + j) * PITCH + p * NG
                work1[pl.ds(start, NG), :] = after_z[j * NG:(j + 1) * NG, p * 128:p * 128 + 128]

    def through_spectrum(at, i):
        for j in range(GROUP2):
            cells = (2 * (i * GROUP2 + j), 2 * (i * GROUP2 + j) + 1)
            pair = [
                jnp.concatenate(
                    [
                        work1[pl.ds(at * SPAN + cell + p * NG, NG, stride=PITCH), :].astype(BF16)
                        for p in range(2)
                    ],
                    axis=0,
                )
                for cell in cells
            ]
            spectrum = dot(forward, jnp.concatenate(pair, axis=1))
            pair = []
            for h, cell in enumerate(cells):
                factor = scale / (base[at] + coul[at, pl.ds(cell, 1), :])
                part = spectrum[:, h * 128:h * 128 + 128]
                pair.append(
                    jnp.concatenate([(part[:NG] * factor).astype(BF16), (part[NG:] * factor).astype(BF16)], axis=0)
                )
            after_y = dot(backward, jnp.concatenate(pair, axis=1))
            for h, cell in enumerate(cells):
                work2[pl.ds(at * SPAN + cell * PITCH, ROWS), :] = after_y[:, h * 128:h * 128 + 128]

    def out_of_spectrum(at, i):
        mixed = [
            jnp.concatenate(
                [
                    work2[pl.ds(at * SPAN + 2 * i * GROUP3 + j + p * NG, NG, stride=PITCH), :].astype(BF16)
                    for p in range(2)
                ],
                axis=1,
            )
            for j in range(2 * GROUP3)
        ]
        after_z = dot(jnp.concatenate(mixed, axis=0), zbackward).astype(BF16)
        for j in range(GROUP3):
            pair = [
                jnp.concatenate([after_z[n * NG:(n + 1) * NG, :128], after_z[n * NG:(n + 1) * NG, 128:]], axis=0)
                for n in (2 * j, 2 * j + 1)
            ]
            potential = dot(backward, jnp.concatenate(pair, axis=1))
            for h in range(2):
                cell = 2 * (i * GROUP3 + j) + h
                s = src[at, cell].astype(F32)
                sr, si = s[:NG], s[NG:]
                pr = potential[:NG, h * 128:h * 128 + 128]
                pi = potential[NG:, h * 128:h * 128 + 128]
                total[cell, :NG, :] += sr * pr - si * pi
                total[cell, NG:, :] += sr * pi + si * pr

    def batch(num, carry):
        lax.fori_loop(num * BATCH, num * BATCH + BATCH, prepare, 0)
        for phase, size in ((into_spectrum, GROUP1), (through_spectrum, GROUP2), (out_of_spectrum, GROUP3)):
            count = NG // 2 // size

            def one(k, carry):
                phase(k // count, k % count)
                return carry

            lax.fori_loop(0, BATCH * count, one, 0)
        return carry

    lax.fori_loop(0, 4 // BATCH, batch, 0)

    for g in range(6):
        for chunk in range(3):
            cells = [8 * g + 2 * chunk + k for k in range(4)]
            narrow = dot(jnp.concatenate([total[n].astype(BF16) for n in cells], axis=1), gather_ref[chunk])
            for p in range(2):
                rows_f32[pl.ds(2 * (3 * g + chunk) + p, NG, stride=36), :] = narrow[p * NG:(p + 1) * NG]

    def to_owner(h, e, z_, k):
        where = device(x, (y + k) % 4, z, e)
        return link(chunks.at[h, e, z_], arrived.at[z_, k], ry_send.at[h, e], ry_recv.at[z_], where)

    order = (4, 3, 5, 2, 6, 1, 7, 0)
    for d in order:
        z_ = (z + d) % 8
        for h in range(2):
            for e in range(2):
                start = 54 * (4 * z_ + 2 * h + e)
                chunks[h, e, z_] = rows_f32[pl.ds(start, 64), :].astype(BF16)

        @pl.when(primary)
        def _():
            to_owner(mine, 1 - c, z_, 0).start()
            for e in range(2):
                to_owner(1 - mine, e, z_, 2).start()
            arrived[z_, 0] = chunks[mine, c, z_]

        @pl.when(secondary)
        def _():
            for e in range(2):
                to_owner(((y + 1) % 4) // 2, e, z_, 1).start()
                to_owner(((y + 3) % 4) // 2, e, z_, 3).start()

    def share(d):
        to_z = (z + d) % 8
        return link(parts.at[to_z], finals.at[d], rz_send.at[d], rz_recv.at[d], device(x, y, to_z, c))

    for d in order:
        z_ = (z + d) % 8

        @pl.when(primary)
        def _():
            three = arrived.at[z_, pl.ds(1, 3)]
            link(three, three, ry_send.at[0, 0], ry_recv.at[z_], other).wait_recv()

        @pl.when(secondary)
        def _():
            link(arrived.at[z_], arrived.at[z_], ry_send.at[0, 0], ry_recv.at[z_], other).wait_recv()

        summed = sum([arrived[z_, k].astype(F32) for k in range(1, 4)], arrived[z_, 0].astype(F32))
        if d:
            parts[z_] = summed.astype(BF16)
            share(d).start()

    for d in range(1, 8):
        share(d).wait_recv()
        summed = summed + finals[d].astype(F32)
    result = summed * (-1.0 / 8.0)
    for k in range(27):
        out_ref[:, 128 * k:128 * k + 128] = result[2 * k:2 * k + 2]

    for d in range(1, 8):
        along_z(d).wait_send()
        share(d).wait_send()
    for n in range(4):
        along_x(n).wait_send()
        across(n).wait_send()
    for n in range(2):
        relay(n).wait_send()
    for d in range(1, 4):
        group(d, 0, 0).wait_send()

    def sent(h, e):
        return link(chunks.at[h, e], chunks.at[h, e], ry_send.at[h, e], ry_recv.at[0], other)

    @pl.when(primary)
    def _():
        sent(mine, 1 - c).wait_send()
        for e in range(2):
            sent(1 - mine, e).wait_send()

    @pl.when(secondary)
    def _():
        group(0, 0, 0).wait_send()
        for h in range(2):
            for e in range(2):
                sent(h, e).wait_send()


def per_device(targets, sources, kpt_coord):
    tables = [jnp.asarray(a) for a in host_tables()]
    vmem = pl.BlockSpec(memory_space=pltpu.VMEM)
    anywhere = pl.BlockSpec(memory_space=pl.ANY)
    sems = pltpu.SemaphoreType.DMA
    out = pl.pallas_call(
        exchange,
        in_specs=[anywhere] * 10,
        out_specs=vmem,
        out_shape=jax.ShapeDtypeStruct((2, 3456), F32),
        scratch_shapes=[
            pltpu.SMEM((3, 8), jnp.int32),
            pltpu.VMEM((2, 3456), BF16),
            pltpu.VMEM((1728, 128), BF16),
        ]
        + [pltpu.VMEM(a.shape, BF16) for a in tables]
        + [
            pltpu.VMEM((64, 128), F32),
            pltpu.VMEM((64, 128), BF16),
            pltpu.VMEM((8, 64, 128), BF16),
            pltpu.VMEM((2, 2, 8, 64, 128), BF16),
            pltpu.VMEM((1744, 128), F32),
            pltpu.VMEM((ROWS, NG * NG), BF16),
            pltpu.VMEM((NG, ROWS, 128), BF16),
            pltpu.VMEM((4, 2, ROWS, NG * NG), BF16),
            pltpu.VMEM((BATCH, NG, ROWS, 128), BF16),
            pltpu.VMEM((BATCH * SPAN, 128), F32),
            pltpu.VMEM((BATCH * SPAN, 128), F32),
            pltpu.VMEM((BATCH, NG, 128), F32),
            pltpu.VMEM((BATCH, NG, 128), F32),
            pltpu.VMEM((NG, ROWS, 128), F32),
            pltpu.VMEM((2, 2, 8, 64, 128), BF16),
            pltpu.VMEM((8, 4, 64, 128), BF16),
            pltpu.VMEM((8, 64, 128), BF16),
            pltpu.VMEM((8, 64, 128), BF16),
            sems((10,)), sems((8,)), sems((8,)), sems((4,)), sems((4, 2)), sems((6,)), sems((6,)),
            sems((4,)), sems((4,)), sems((2, 2)), sems((8,)), sems((8,)), sems((8,)),
        ],
        compiler_params=pltpu.CompilerParams(
            collective_id=0, has_side_effects=True, vmem_limit_bytes=62 * 2**20
        ),
    )(
        kpt_coord.T,
        targets.reshape(2, 3456),
        sources.reshape(2, 864, 128).transpose(1, 0, 2).reshape(1728, 128),
        *tables,
    )
    return out.reshape(1, 1, 2, 3456)


def solution(mesh):
    in_specs = (P("kpt", None, None, "band"), P("kpt", "band", None, None), P())
    out_specs = P("kpt", None, None, "band")
    return jax.shard_map(per_device, mesh=mesh, in_specs=in_specs, out_specs=out_specs, check_vma=False)
```

```python
import functools
import math

import jax
import jax.numpy as jnp
import ml_dtypes
import numpy as np
from jax import lax
from jax.experimental import pallas as pl
from jax.experimental.pallas import tpu as pltpu
from jax.sharding import PartitionSpec as P

NG = 48
ROWS = 2 * NG
PITCH = 104
GROUP1 = 24
GROUP2 = 24
GROUP3 = 24
BATCH = 2
SPAN = NG * PITCH
SPREAD_FROM = (0, 0, 128, 256)
SPREAD_WIDE = (128, 256, 256, 128)
BF16 = jnp.bfloat16
F32 = jnp.float32
MESH = pl.DeviceIdType.MESH


def host_tables():
    index = np.arange(NG)
    phases = ((index[:, None] * index[None, :]) % NG).astype(np.float32) * np.float32(2.0 * math.pi / NG)
    half_type = ml_dtypes.bfloat16
    cosine = np.cos(phases).astype(half_type).astype(np.float32)
    sine = np.sin(phases).astype(half_type).astype(np.float32)
    forward = np.block([[cosine, sine], [-sine, cosine]])
    backward = np.block([[cosine, -sine], [sine, cosine]])

    def lane_table(table):
        wide = np.zeros((2, 2, 64, 2, 2, 64), np.float32)
        for p in range(2):
            for q in range(2):
                for t in range(2):
                    wide[p, t, :NG, q, t, :NG] = table[q * NG:(q + 1) * NG, p * NG:(p + 1) * NG].T
        return wide.reshape(256, 256)

    one = np.zeros((4, 256, 2, 2, 64), np.float32)
    two = np.zeros((4, 512, 2, 2, 64), np.float32)
    gather = np.zeros((3, 4, 2, 64, 128), np.float32)
    for k in range(8):
        lanes = slice(48 * k - SPREAD_FROM[k // 2], 48 * (k + 1) - SPREAD_FROM[k // 2])
        width = SPREAD_WIDE[k // 2]
        for half in range(2):
            one[k // 2, lanes, k % 2, half, :NG] = np.eye(NG)
            two[k // 2, lanes.start + half * width:lanes.stop + half * width, k % 2, half, :NG] = np.eye(NG)
            for chunk in range(3):
                for z in range(NG):
                    lane = 48 * k + z - 128 * chunk
                    if 0 <= lane < 128:
                        gather[chunk, k - 2 * chunk, half, z, lane] = 1
    return [
        a.astype(half_type)
        for a in (
            forward,
            backward,
            lane_table(forward),
            lane_table(backward),
            one.reshape(4, 256, 256),
            two.reshape(4, 512, 256),
            gather.reshape(3, 512, 128),
        )
    ]


def dot(a, b):
    return jnp.dot(a, b, preferred_element_type=F32)


def exchange(
    kpt_hbm, slice_hbm, source_hbm, fwd_hbm, bwd_hbm, zfwd_hbm, zbwd_hbm, one_hbm, two_hbm, gather_hbm, out_ref,
    kpt_ref, slice_ref, raw_ref, fwd_ref, bwd_ref, zfwd_ref, zbwd_ref, one_ref, two_ref, gather_ref,
    staged, piece, carried, slots, rows_f32, dense, targ, sources, src, work1, work2, coul, base, total,
    chunks, arrived, parts, finals,
    in_sem, gz_send, gz_recv, gy_send, gy_recv, s_send, s_recv, c_send, c_recv,
    ry_send, ry_recv, rz_send, rz_recv,
):
    kpt = lax.axis_index("kpt")
    band = lax.axis_index("band")
    x = kpt % 4
    y = (kpt // 4) + ((band // 2) % 2) * 2
    z = band // 4
    c = band % 2
    mine = y // 2
    primary = c == y % 2
    secondary = c != y % 2

    def device(x_, y_, z_, c_):
        return ((y_ % 2) * 4 + x_, z_ * 4 + (y_ // 2) * 2 + c_)

    def link(source, target, send, recv, where):
        return pltpu.make_async_remote_copy(
            src_ref=source, dst_ref=target, send_sem=send, recv_sem=recv, device_id=where, device_id_type=MESH
        )

    x_up = device((x + 1) % 4, y, z, c)
    x_down = device((x + 3) % 4, y, z, c)
    other = device(x, y, z, 1 - c)

    fetched = [
        pltpu.make_async_copy(a, b, in_sem.at[i])
        for i, (a, b) in enumerate(
            (
                (slice_hbm, slice_ref), (source_hbm, raw_ref), (kpt_hbm, kpt_ref), (one_hbm, one_ref),
                (two_hbm, two_ref), (fwd_hbm, fwd_ref), (bwd_hbm, bwd_ref), (zfwd_hbm, zfwd_ref),
                (zbwd_hbm, zbwd_ref), (gather_hbm, gather_ref),
            )
        )
    ]
    for copy in fetched:
        copy.start()

    barrier = pltpu.get_barrier_semaphore()
    peers = [x_up, x_down, other] + [device(x, y, (z + d) % 8, c) for d in range(1, 8)]
    peers += [device(x, (y + d) % 4, z, e) for d in range(1, 4) for e in range(2)]
    for peer in peers:
        pl.semaphore_signal(barrier, inc=1, device_id=peer, device_id_type=MESH)

    fetched[0].wait()
    for k in range(27):
        staged[2 * k:2 * k + 2, :] = slice_ref[:, 128 * k:128 * k + 128].astype(F32)
    piece[...] = staged[...].astype(BF16)

    pl.semaphore_wait(barrier, len(peers))

    def along_z(d):
        return link(piece, carried.at[z], gz_send.at[d], gz_recv.at[d], device(x, y, (z + d) % 8, c))

    def along_y(d, held, z_):
        return link(
            held, slots.at[mine, c, z_], gy_send.at[d], gy_recv.at[d, c], device(x, (y + d) % 4, z, y % 2)
        )

    def spread_y(held, z_):
        for d in range(1, 4):
            along_y(d, held, z_).start()

        @pl.when(secondary)
        def _():
            along_y(0, held, z_).start()

    for d in (4, 3, 5, 2, 6, 1, 7):
        along_z(d).start()
    spread_y(piece, z)

    fetched[1].wait()

    def densify(raw, store):
        for p in range(2):
            for col in range(18):
                store(p, col, raw[pl.ds(2 * col + p, NG, stride=36), :].astype(BF16))

    rows_f32[pl.ds(0, 2 * 864), :] = raw_ref[...].astype(F32)

    def keep_source(p, col, block):
        sources[0, c, p * NG:(p + 1) * NG, col * 128:(col + 1) * 128] = block

    densify(rows_f32, keep_source)

    low = pl.ds(0, NG)
    high = pl.ds(NG, NG)
    legs = ((low, 1, x_up), (high, 2, x_down), (high, 1, x_up), (low, 2, x_down))

    def along_x(n):
        part, place, to = legs[n]
        return link(sources.at[0, c, part], sources.at[place, c, part], s_send.at[n], s_recv.at[n], to)

    def relay(n):
        part, place, to = legs[n]
        return link(sources.at[place, c, part], sources.at[3, c, part], s_send.at[4 + n], s_recv.at[4 + n], to)

    def across(n):
        held = sources.at[0, c] if n == 6 else sources.at[(1, 2, 1, 2, 3, 3)[n], c, (low, high)[(0, 1, 1, 0, 0, 1)[n]]]
        return link(held, held, c_send.at[n], c_recv.at[n], other)

    for n in range(4):
        along_x(n).start()
    across(6).start()
    total[...] = jnp.zeros_like(total)

    for d in (1, 7, 2, 6, 3, 5, 4):
        along_z(d).wait_recv()
        from_z = (z + 8 - d) % 8
        spread_y(carried.at[from_z], from_z)

    for n in range(2):
        along_x(n).wait_recv()
        across(n).start()

    def group(d, h, e):
        whole = slots.at[h, e]
        return link(whole, whole, gy_send.at[d], gy_recv.at[d, e], other)

    @pl.when(primary)
    def _():
        carried[z] = piece[...]
        slots[mine, c] = carried[...]
        group(0, mine, 1 - c).wait_recv()
        for e in range(2):
            group(2, 1 - mine, e).wait_recv()

    @pl.when(secondary)
    def _():
        for e in range(2):
            group(1, ((y + 3) % 4) // 2, e).wait_recv()
            group(3, ((y + 1) % 4) // 2, e).wait_recv()

    def unpack(z_, carry):
        for h in range(2):
            for e in range(2):
                start = 54 * (4 * z_ + 2 * h + e)
                rows_f32[pl.ds(start, 54), :] = slots[h, e, z_].astype(F32)[:54]
        return carry

    lax.fori_loop(0, 8, unpack, 0)

    def keep_target(p, col, block):
        dense[p * NG:(p + 1) * NG, col * 128:(col + 1) * 128] = block

    densify(rows_f32, keep_target)

    for copy in fetched[2:]:
        copy.wait()
    for n in range(2, 4):
        along_x(n).wait_recv()
        across(n).start()
    for n in range(2):
        relay(n).start()

    def spread_out(read, table, copies, store):
        for g in range(6):
            for k in range(4):
                width = SPREAD_WIDE[k]
                lanes = slice(384 * g + SPREAD_FROM[k], 384 * g + SPREAD_FROM[k] + width)
                rows = [read(i, lanes) for i in range(copies)]
                wide = dot(rows[0] if copies == 1 else jnp.concatenate(rows, axis=1), table[k, :copies * width, :])
                wide = wide.astype(BF16)
                store(8 * g + 2 * k, wide[:, :128])
                store(8 * g + 2 * k + 1, wide[:, 128:])

    def set_target(cell, block):
        targ[cell] = block

    spread_out(lambda i, lanes: dense[:, lanes], one_ref, 1, set_target)

    lane = lax.broadcasted_iota(jnp.int32, (NG, 128), 1)
    row = lax.broadcasted_iota(jnp.int32, (NG, 128), 0)

    def frequency(i):
        return jnp.where(i < NG // 2, i, i - NG).astype(F32)

    scale = 4.0 * math.pi / float(NG**3)
    forward = fwd_ref[...]
    backward = bwd_ref[...]
    zforward = zfwd_ref[...]
    zbackward = zbwd_ref[...]

    def prepare(num, carry):
        for place, needed in enumerate(((6,), (0, 2), (1, 3), (4, 5))):

            @pl.when(num == place)
            def _():
                for n in needed:
                    across(n).wait_recv()

        at = num % BATCH

        def set_source(cell, block):
            src[at, cell] = block

        spread_out(lambda i, lanes: sources[num, i, :, lanes], two_ref, 2, set_source)
        from_x = jnp.where(num == 0, 0, jnp.where(num == 1, 3, jnp.where(num == 2, 1, 2)))
        from_k = (kpt // 4) * 4 + (x + from_x) % 4

        def offset(d):
            return (kpt_ref[d, c * 4 + x] - kpt_ref[d, from_k]).astype(F32) * 0.25

        fx = frequency(row) + offset(0)
        fy = frequency(row) + offset(1)
        fz = frequency(lane % 64) + offset(2)
        coul[at] = 0.04 * (fx * fx)
        base[at] = 0.04 * (fy * fy + fz * fz) + 0.25
        return carry

    def into_spectrum(at, i):
        mixed = []
        for j in range(GROUP1):
            pair = []
            for cell in (2 * (i * GROUP1 + j), 2 * (i * GROUP1 + j) + 1):
                s = src[at, cell].astype(F32)
                t = targ[cell].astype(F32)
                sr, si, tr, ti = s[:NG], s[NG:], t[:NG], t[NG:]
                pair.append(
                    jnp.concatenate([(sr * tr + si * ti).astype(BF16), (sr * ti - si * tr).astype(BF16)], axis=0)
                )
            after_x = dot(forward, jnp.concatenate(pair, axis=1)).astype(BF16)
            for h in (0, 128):
                mixed.append(jnp.concatenate([after_x[:NG, h:h + 128], after_x[NG:, h:h + 128]], axis=1))
        after_z = dot(jnp.concatenate(mixed, axis=0), zforward)
        for j in range(2 * GROUP1):
            for p in range(2):
                start = at * SPAN + (2 * i * GROUP1 + j) * PITCH + p * NG
                work1[pl.ds(start, NG), :] = after_z[j * NG:(j + 1) * NG, p * 128:p * 128 + 128]

    def through_spectrum(at, i):
        for j in range(GROUP2):
            cells = (2 * (i * GROUP2 + j), 2 * (i * GROUP2 + j) + 1)
            pair = [
                jnp.concatenate(
                    [
                        work1[pl.ds(at * SPAN + cell + p * NG, NG, stride=PITCH), :].astype(BF16)
                        for p in range(2)
                    ],
                    axis=0,
                )
                for cell in cells
            ]
            spectrum = dot(forward, jnp.concatenate(pair, axis=1))
            pair = []
            for h, cell in enumerate(cells):
                factor = scale / (base[at] + coul[at, pl.ds(cell, 1), :])
                part = spectrum[:, h * 128:h * 128 + 128]
                pair.append(
                    jnp.concatenate([(part[:NG] * factor).astype(BF16), (part[NG:] * factor).astype(BF16)], axis=0)
                )
            after_y = dot(backward, jnp.concatenate(pair, axis=1))
            for h, cell in enumerate(cells):
                work2[pl.ds(at * SPAN + cell * PITCH, ROWS), :] = after_y[:, h * 128:h * 128 + 128]

    def out_of_spectrum(at, i):
        mixed = [
            jnp.concatenate(
                [
                    work2[pl.ds(at * SPAN + 2 * i * GROUP3 + j + p * NG, NG, stride=PITCH), :].astype(BF16)
                    for p in range(2)
                ],
                axis=1,
            )
            for j in range(2 * GROUP3)
        ]
        after_z = dot(jnp.concatenate(mixed, axis=0), zbackward).astype(BF16)
        for j in range(GROUP3):
            pair = [
                jnp.concatenate([after_z[n * NG:(n + 1) * NG, :128], after_z[n * NG:(n + 1) * NG, 128:]], axis=0)
                for n in (2 * j, 2 * j + 1)
            ]
            potential = dot(backward, jnp.concatenate(pair, axis=1))
            for h in range(2):
                cell = 2 * (i * GROUP3 + j) + h
                s = src[at, cell].astype(F32)
                sr, si = s[:NG], s[NG:]
                pr = potential[:NG, h * 128:h * 128 + 128]
                pi = potential[NG:, h * 128:h * 128 + 128]
                total[cell, :NG, :] += sr * pr - si * pi
                total[cell, NG:, :] += sr * pi + si * pr

    def batch(num, carry):
        lax.fori_loop(num * BATCH, num * BATCH + BATCH, prepare, 0)
        for phase, size in ((into_spectrum, GROUP1), (through_spectrum, GROUP2), (out_of_spectrum, GROUP3)):
            count = NG // 2 // size

            def one(k, carry):
                phase(k // count, k % count)
                return carry

            lax.fori_loop(0, BATCH * count, one, 0)

            if phase is through_spectrum:

                @pl.when(num == 0)
                def _():
                    for n in range(2):
                        relay(n).wait_recv()
                        across(4 + n).start()

        return carry

    lax.fori_loop(0, 4 // BATCH, batch, 0)

    for g in range(6):
        for chunk in range(3):
            cells = [8 * g + 2 * chunk + k for k in range(4)]
            narrow = dot(jnp.concatenate([total[n].astype(BF16) for n in cells], axis=1), gather_ref[chunk])
            for p in range(2):
                rows_f32[pl.ds(2 * (3 * g + chunk) + p, NG, stride=36), :] = narrow[p * NG:(p + 1) * NG]

    def to_owner(h, e, z_, k):
        where = device(x, (y + k) % 4, z, e)
        return link(chunks.at[h, e, z_], arrived.at[z_, k], ry_send.at[h, e], ry_recv.at[z_], where)

    order = (4, 3, 5, 2, 6, 1, 7, 0)
    for d in order:
        z_ = (z + d) % 8
        for h in range(2):
            for e in range(2):
                start = 54 * (4 * z_ + 2 * h + e)
                chunks[h, e, z_] = rows_f32[pl.ds(start, 64), :].astype(BF16)

        @pl.when(primary)
        def _():
            to_owner(mine, 1 - c, z_, 0).start()
            for e in range(2):
                to_owner(1 - mine, e, z_, 2).start()
            arrived[z_, 0] = chunks[mine, c, z_]

        @pl.when(secondary)
        def _():
            for e in range(2):
                to_owner(((y + 1) % 4) // 2, e, z_, 1).start()
                to_owner(((y + 3) % 4) // 2, e, z_, 3).start()

    def share(d):
        to_z = (z + d) % 8
        return link(parts.at[to_z], finals.at[d], rz_send.at[d], rz_recv.at[d], device(x, y, to_z, c))

    for d in order:
        z_ = (z + d) % 8

        @pl.when(primary)
        def _():
            three = arrived.at[z_, pl.ds(1, 3)]
            link(three, three, ry_send.at[0, 0], ry_recv.at[z_], other).wait_recv()

        @pl.when(secondary)
        def _():
            link(arrived.at[z_], arrived.at[z_], ry_send.at[0, 0], ry_recv.at[z_], other).wait_recv()

        summed = sum([arrived[z_, k].astype(F32) for k in range(1, 4)], arrived[z_, 0].astype(F32))
        if d:
            parts[z_] = summed.astype(BF16)
            share(d).start()

    for d in range(1, 8):
        share(d).wait_recv()
        summed = summed + finals[d].astype(F32)
    result = summed * (-1.0 / 8.0)
    for k in range(27):
        out_ref[:, 128 * k:128 * k + 128] = result[2 * k:2 * k + 2]

    for d in range(1, 8):
        along_z(d).wait_send()
        share(d).wait_send()
    for n in range(4):
        along_x(n).wait_send()
    for n in range(7):
        across(n).wait_send()
    for n in range(2):
        relay(n).wait_send()
    for d in range(1, 4):
        group(d, 0, 0).wait_send()

    def sent(h, e):
        return link(chunks.at[h, e], chunks.at[h, e], ry_send.at[h, e], ry_recv.at[0], other)

    @pl.when(primary)
    def _():
        sent(mine, 1 - c).wait_send()
        for e in range(2):
            sent(1 - mine, e).wait_send()

    @pl.when(secondary)
    def _():
        group(0, 0, 0).wait_send()
        for h in range(2):
            for e in range(2):
                sent(h, e).wait_send()


def per_device(targets, sources, kpt_coord):
    tables = [jnp.asarray(a) for a in host_tables()]
    vmem = pl.BlockSpec(memory_space=pltpu.VMEM)
    anywhere = pl.BlockSpec(memory_space=pl.ANY)
    sems = pltpu.SemaphoreType.DMA
    out = pl.pallas_call(
        exchange,
        in_specs=[anywhere] * 10,
        out_specs=vmem,
        out_shape=jax.ShapeDtypeStruct((2, 3456), F32),
        scratch_shapes=[
            pltpu.SMEM((3, 8), jnp.int32),
            pltpu.VMEM((2, 3456), BF16),
            pltpu.VMEM((1728, 128), BF16),
        ]
        + [pltpu.VMEM(a.shape, BF16) for a in tables]
        + [
            pltpu.VMEM((64, 128), F32),
            pltpu.VMEM((64, 128), BF16),
            pltpu.VMEM((8, 64, 128), BF16),
            pltpu.VMEM((2, 2, 8, 64, 128), BF16),
            pltpu.VMEM((1744, 128), F32),
            pltpu.VMEM((ROWS, NG * NG), BF16),
            pltpu.VMEM((NG, ROWS, 128), BF16),
            pltpu.VMEM((4, 2, ROWS, NG * NG), BF16),
            pltpu.VMEM((BATCH, NG, ROWS, 128), BF16),
            pltpu.VMEM((BATCH * SPAN, 128), F32),
            pltpu.VMEM((BATCH * SPAN, 128), F32),
            pltpu.VMEM((BATCH, NG, 128), F32),
            pltpu.VMEM((BATCH, NG, 128), F32),
            pltpu.VMEM((NG, ROWS, 128), F32),
            pltpu.VMEM((2, 2, 8, 64, 128), BF16),
            pltpu.VMEM((8, 4, 64, 128), BF16),
            pltpu.VMEM((8, 64, 128), BF16),
            pltpu.VMEM((8, 64, 128), BF16),
            sems((10,)), sems((8,)), sems((8,)), sems((4,)), sems((4, 2)), sems((6,)), sems((6,)),
            sems((7,)), sems((7,)), sems((2, 2)), sems((8,)), sems((8,)), sems((8,)),
        ],
        compiler_params=pltpu.CompilerParams(
            collective_id=0, has_side_effects=True, vmem_limit_bytes=62 * 2**20
        ),
    )(
        kpt_coord.T,
        targets.reshape(2, 3456),
        sources.reshape(2, 864, 128).transpose(1, 0, 2).reshape(1728, 128),
        *tables,
    )
    return out.reshape(1, 1, 2, 3456)


def solution(mesh):
    in_specs = (P("kpt", None, None, "band"), P("kpt", "band", None, None), P())
    out_specs = P("kpt", None, None, "band")
    return jax.shard_map(per_device, mesh=mesh, in_specs=in_specs, out_specs=out_specs, check_vma=False)
```

```python
import functools
import math

import jax
import jax.numpy as jnp
import ml_dtypes
import numpy as np
from jax import lax
from jax.experimental import pallas as pl
from jax.experimental.pallas import tpu as pltpu
from jax.sharding import PartitionSpec as P

NG = 48
ROWS = 2 * NG
PITCH = 104
GROUP1 = 24
GROUP2 = 24
GROUP3 = 24
BATCH = 4
SPAN = NG * PITCH
SPREAD_FROM = (0, 0, 128, 256)
SPREAD_WIDE = (128, 256, 256, 128)
BF16 = jnp.bfloat16
F32 = jnp.float32
MESH = pl.DeviceIdType.MESH


def host_tables():
    index = np.arange(NG)
    phases = ((index[:, None] * index[None, :]) % NG).astype(np.float32) * np.float32(2.0 * math.pi / NG)
    half_type = ml_dtypes.bfloat16
    cosine = np.cos(phases).astype(half_type).astype(np.float32)
    sine = np.sin(phases).astype(half_type).astype(np.float32)
    forward = np.block([[cosine, sine], [-sine, cosine]])
    backward = np.block([[cosine, -sine], [sine, cosine]])

    def lane_table(table):
        wide = np.zeros((2, 2, 64, 2, 2, 64), np.float32)
        for p in range(2):
            for q in range(2):
                for t in range(2):
                    wide[p, t, :NG, q, t, :NG] = table[q * NG:(q + 1) * NG, p * NG:(p + 1) * NG].T
        return wide.reshape(256, 256)

    one = np.zeros((4, 256, 2, 2, 64), np.float32)
    two = np.zeros((4, 512, 2, 2, 64), np.float32)
    gather = np.zeros((3, 4, 2, 64, 128), np.float32)
    for k in range(8):
        lanes = slice(48 * k - SPREAD_FROM[k // 2], 48 * (k + 1) - SPREAD_FROM[k // 2])
        width = SPREAD_WIDE[k // 2]
        for half in range(2):
            one[k // 2, lanes, k % 2, half, :NG] = np.eye(NG)
            two[k // 2, lanes.start + half * width:lanes.stop + half * width, k % 2, half, :NG] = np.eye(NG)
            for chunk in range(3):
                for z in range(NG):
                    lane = 48 * k + z - 128 * chunk
                    if 0 <= lane < 128:
                        gather[chunk, k - 2 * chunk, half, z, lane] = 1
    return [
        a.astype(half_type)
        for a in (
            forward,
            backward,
            lane_table(forward),
            lane_table(backward),
            one.reshape(4, 256, 256),
            two.reshape(4, 512, 256),
            gather.reshape(3, 512, 128),
        )
    ]


def dot(a, b):
    return jnp.dot(a, b, preferred_element_type=F32)


def exchange(
    kpt_hbm, slice_hbm, source_hbm, fwd_hbm, bwd_hbm, zfwd_hbm, zbwd_hbm, one_hbm, two_hbm, gather_hbm, out_ref,
    kpt_ref, slice_ref, raw_ref, fwd_ref, bwd_ref, zfwd_ref, zbwd_ref, one_ref, two_ref, gather_ref,
    staged, piece, carried, slots, rows_f32, dense, targ, sources, src, work1, work2, coul, base, total,
    chunks, arrived, parts, finals,
    in_sem, gz_send, gz_recv, gy_send, gy_recv, s_send, s_recv, c_send, c_recv,
    ry_send, ry_recv, rz_send, rz_recv,
):
    kpt = lax.axis_index("kpt")
    band = lax.axis_index("band")
    x = kpt % 4
    y = (kpt // 4) + ((band // 2) % 2) * 2
    z = band // 4
    c = band % 2
    mine = y // 2
    primary = c == y % 2
    secondary = c != y % 2

    def device(x_, y_, z_, c_):
        return ((y_ % 2) * 4 + x_, z_ * 4 + (y_ // 2) * 2 + c_)

    def link(source, target, send, recv, where):
        return pltpu.make_async_remote_copy(
            src_ref=source, dst_ref=target, send_sem=send, recv_sem=recv, device_id=where, device_id_type=MESH
        )

    x_up = device((x + 1) % 4, y, z, c)
    x_down = device((x + 3) % 4, y, z, c)
    other = device(x, y, z, 1 - c)

    fetched = [
        pltpu.make_async_copy(a, b, in_sem.at[i])
        for i, (a, b) in enumerate(
            (
                (slice_hbm, slice_ref), (source_hbm, raw_ref), (kpt_hbm, kpt_ref), (one_hbm, one_ref),
                (two_hbm, two_ref), (fwd_hbm, fwd_ref), (bwd_hbm, bwd_ref), (zfwd_hbm, zfwd_ref),
                (zbwd_hbm, zbwd_ref), (gather_hbm, gather_ref),
            )
        )
    ]
    for copy in fetched:
        copy.start()

    barrier = pltpu.get_barrier_semaphore()
    peers = [x_up, x_down, other] + [device(x, y, (z + d) % 8, c) for d in range(1, 8)]
    peers += [device(x, (y + d) % 4, z, e) for d in range(1, 4) for e in range(2)]
    for peer in peers:
        pl.semaphore_signal(barrier, inc=1, device_id=peer, device_id_type=MESH)

    fetched[0].wait()
    for k in range(27):
        staged[2 * k:2 * k + 2, :] = slice_ref[:, 128 * k:128 * k + 128].astype(F32)
    piece[...] = staged[...].astype(BF16)

    fetched[1].wait()

    def densify(raw, store):
        for p in range(2):
            for col in range(18):
                store(p, col, raw[pl.ds(2 * col + p, NG, stride=36), :].astype(BF16))

    rows_f32[pl.ds(0, 2 * 864), :] = raw_ref[...].astype(F32)

    def keep_source(p, col, block):
        sources[0, c, p * NG:(p + 1) * NG, col * 128:(col + 1) * 128] = block

    densify(rows_f32, keep_source)

    pl.semaphore_wait(barrier, len(peers))

    def along_z(d):
        return link(piece, carried.at[z], gz_send.at[d], gz_recv.at[d], device(x, y, (z + d) % 8, c))

    def along_y(d, held, z_):
        return link(
            held, slots.at[mine, c, z_], gy_send.at[d], gy_recv.at[d, c], device(x, (y + d) % 4, z, y % 2)
        )

    def spread_y(held, z_):
        for d in range(1, 4):
            along_y(d, held, z_).start()

        @pl.when(secondary)
        def _():
            along_y(0, held, z_).start()

    for d in (4, 3, 5, 2, 6, 1, 7):
        along_z(d).start()
    low = pl.ds(0, NG)
    high = pl.ds(NG, NG)
    legs = ((low, 1, x_up), (high, 2, x_down), (high, 1, x_up), (low, 2, x_down))

    def along_x(n):
        part, place, to = legs[n]
        return link(sources.at[0, c, part], sources.at[place, c, part], s_send.at[n], s_recv.at[n], to)

    def relay(n):
        part, place, to = legs[n]
        return link(sources.at[place, c, part], sources.at[3, c, part], s_send.at[4 + n], s_recv.at[4 + n], to)

    def across(n):
        held = sources.at[0, c] if n == 6 else sources.at[(1, 2, 1, 2, 3, 3)[n], c, (low, high)[(0, 1, 1, 0, 0, 1)[n]]]
        return link(held, held, c_send.at[n], c_recv.at[n], other)

    for n in range(4):
        along_x(n).start()
    spread_y(piece, z)
    across(6).start()
    total[...] = jnp.zeros_like(total)

    for d in (1, 7, 2, 6, 3, 5, 4):
        along_z(d).wait_recv()
        from_z = (z + 8 - d) % 8
        spread_y(carried.at[from_z], from_z)

    for n in range(2):
        along_x(n).wait_recv()
        across(n).start()

    for copy in fetched[2:]:
        copy.wait()

    def spread_out(read, table, copies, store):
        for g in range(6):
            for k in range(4):
                width = SPREAD_WIDE[k]
                lanes = slice(384 * g + SPREAD_FROM[k], 384 * g + SPREAD_FROM[k] + width)
                rows = [read(i, lanes) for i in range(copies)]
                wide = dot(rows[0] if copies == 1 else jnp.concatenate(rows, axis=1), table[k, :copies * width, :])
                wide = wide.astype(BF16)
                store(8 * g + 2 * k, wide[:, :128])
                store(8 * g + 2 * k + 1, wide[:, 128:])

    lane = lax.broadcasted_iota(jnp.int32, (NG, 128), 1)
    row = lax.broadcasted_iota(jnp.int32, (NG, 128), 0)

    def frequency(i):
        return jnp.where(i < NG // 2, i, i - NG).astype(F32)

    scale = 4.0 * math.pi / float(NG**3)

    def prepare(num):
        for place, needed in enumerate(((6,), (0, 2), (1, 3), (4, 5))):

            @pl.when(jnp.equal(num, place))
            def _():
                for n in needed:
                    across(n).wait_recv()

        at = num

        def set_source(cell, block):
            src[at, cell] = block

        spread_out(lambda i, lanes: sources[num, i, :, lanes], two_ref, 2, set_source)
        from_x = jnp.where(num == 0, 0, jnp.where(num == 1, 3, jnp.where(num == 2, 1, 2)))
        from_k = (kpt // 4) * 4 + (x + from_x) % 4

        def offset(d):
            return (kpt_ref[d, c * 4 + x] - kpt_ref[d, from_k]).astype(F32) * 0.25

        fx = frequency(row) + offset(0)
        fy = frequency(row) + offset(1)
        fz = frequency(lane % 64) + offset(2)
        coul[at] = 0.04 * (fx * fx)
        base[at] = 0.04 * (fy * fy + fz * fz) + 0.25

    prepare(0)
    forward = fwd_ref[...]
    backward = bwd_ref[...]
    zforward = zfwd_ref[...]
    zbackward = zbwd_ref[...]

    def group(d, h, e):
        whole = slots.at[h, e]
        return link(whole, whole, gy_send.at[d], gy_recv.at[d, e], other)

    @pl.when(primary)
    def _():
        carried[z] = piece[...]
        slots[mine, c] = carried[...]
        group(0, mine, 1 - c).wait_recv()
        for e in range(2):
            group(2, 1 - mine, e).wait_recv()

    @pl.when(secondary)
    def _():
        for e in range(2):
            group(1, ((y + 3) % 4) // 2, e).wait_recv()
            group(3, ((y + 1) % 4) // 2, e).wait_recv()

    def unpack(z_, carry):
        for h in range(2):
            for e in range(2):
                start = 54 * (4 * z_ + 2 * h + e)
                rows_f32[pl.ds(start, 54), :] = slots[h, e, z_].astype(F32)[:54]
        return carry

    lax.fori_loop(0, 8, unpack, 0)

    def keep_target(p, col, block):
        dense[p * NG:(p + 1) * NG, col * 128:(col + 1) * 128] = block

    densify(rows_f32, keep_target)

    for n in range(2, 4):
        along_x(n).wait_recv()
        across(n).start()
    for n in range(2):
        relay(n).start()

    def set_target(cell, block):
        targ[cell] = block

    spread_out(lambda i, lanes: dense[:, lanes], one_ref, 1, set_target)

    def into_spectrum(at, i):
        mixed = []
        for j in range(GROUP1):
            pair = []
            for cell in (2 * (i * GROUP1 + j), 2 * (i * GROUP1 + j) + 1):
                s = src[at, cell].astype(F32)
                t = targ[cell].astype(F32)
                sr, si, tr, ti = s[:NG], s[NG:], t[:NG], t[NG:]
                pair.append(
                    jnp.concatenate([(sr * tr + si * ti).astype(BF16), (sr * ti - si * tr).astype(BF16)], axis=0)
                )
            after_x = dot(forward, jnp.concatenate(pair, axis=1)).astype(BF16)
            for h in (0, 128):
                mixed.append(jnp.concatenate([after_x[:NG, h:h + 128], after_x[NG:, h:h + 128]], axis=1))
        after_z = dot(jnp.concatenate(mixed, axis=0), zforward)
        for j in range(2 * GROUP1):
            for p in range(2):
                start = at * SPAN + (2 * i * GROUP1 + j) * PITCH + p * NG
                work1[pl.ds(start, NG), :] = after_z[j * NG:(j + 1) * NG, p * 128:p * 128 + 128]

    def through_spectrum(at, i):
        for j in range(GROUP2):
            cells = (2 * (i * GROUP2 + j), 2 * (i * GROUP2 + j) + 1)
            pair = [
                jnp.concatenate(
                    [
                        work1[pl.ds(at * SPAN + cell + p * NG, NG, stride=PITCH), :].astype(BF16)
                        for p in range(2)
                    ],
                    axis=0,
                )
                for cell in cells
            ]
            spectrum = dot(forward, jnp.concatenate(pair, axis=1))
            pair = []
            for h, cell in enumerate(cells):
                factor = scale / (base[at] + coul[at, pl.ds(cell, 1), :])
                part = spectrum[:, h * 128:h * 128 + 128]
                pair.append(
                    jnp.concatenate([(part[:NG] * factor).astype(BF16), (part[NG:] * factor).astype(BF16)], axis=0)
                )
            after_y = dot(backward, jnp.concatenate(pair, axis=1))
            for h, cell in enumerate(cells):
                work2[pl.ds(at * SPAN + cell * PITCH, ROWS), :] = after_y[:, h * 128:h * 128 + 128]

    def out_of_spectrum(at, i):
        mixed = [
            jnp.concatenate(
                [
                    work2[pl.ds(at * SPAN + 2 * i * GROUP3 + j + p * NG, NG, stride=PITCH), :].astype(BF16)
                    for p in range(2)
                ],
                axis=1,
            )
            for j in range(2 * GROUP3)
        ]
        after_z = dot(jnp.concatenate(mixed, axis=0), zbackward).astype(BF16)
        for j in range(GROUP3):
            pair = [
                jnp.concatenate([after_z[n * NG:(n + 1) * NG, :128], after_z[n * NG:(n + 1) * NG, 128:]], axis=0)
                for n in (2 * j, 2 * j + 1)
            ]
            potential = dot(backward, jnp.concatenate(pair, axis=1))
            for h in range(2):
                cell = 2 * (i * GROUP3 + j) + h
                s = src[at, cell].astype(F32)
                sr, si = s[:NG], s[NG:]
                pr = potential[:NG, h * 128:h * 128 + 128]
                pi = potential[NG:, h * 128:h * 128 + 128]
                total[cell, :NG, :] += sr * pr - si * pi
                total[cell, NG:, :] += sr * pi + si * pr

    def begin(num, carry):
        @pl.when(num > 0)
        def _():
            prepare(num)

        for i in range(NG // 2 // GROUP1):
            into_spectrum(num, i)
        return carry

    def middle(num, carry):
        @pl.when(num == 2)
        def _():
            for n in range(2):
                relay(n).wait_recv()
                across(4 + n).start()

        for i in range(NG // 2 // GROUP2):
            through_spectrum(num, i)
        return carry

    def finish(num, carry):
        for i in range(NG // 2 // GROUP3):
            out_of_spectrum(num, i)
        return carry

    def stage(num, carry):
        start, stop = 3 * num, 3 + num
        lax.fori_loop(start, stop, begin, 0)
        lax.fori_loop(start, stop, middle, 0)
        return carry

    lax.fori_loop(0, 2, stage, 0)
    lax.fori_loop(0, 4, finish, 0)

    for g in range(6):
        for chunk in range(3):
            cells = [8 * g + 2 * chunk + k for k in range(4)]
            narrow = dot(jnp.concatenate([total[n].astype(BF16) for n in cells], axis=1), gather_ref[chunk])
            for p in range(2):
                rows_f32[pl.ds(2 * (3 * g + chunk) + p, NG, stride=36), :] = narrow[p * NG:(p + 1) * NG]

    def to_owner(h, e, z_, k):
        where = device(x, (y + k) % 4, z, e)
        return link(chunks.at[h, e, z_], arrived.at[z_, k], ry_send.at[h, e], ry_recv.at[z_], where)

    order = (4, 3, 5, 2, 6, 1, 7, 0)
    for d in order:
        z_ = (z + d) % 8
        for h in range(2):
            for e in range(2):
                start = 54 * (4 * z_ + 2 * h + e)
                chunks[h, e, z_] = rows_f32[pl.ds(start, 64), :].astype(BF16)

        @pl.when(primary)
        def _():
            to_owner(mine, 1 - c, z_, 0).start()
            for e in range(2):
                to_owner(1 - mine, e, z_, 2).start()
            arrived[z_, 0] = chunks[mine, c, z_]

        @pl.when(secondary)
        def _():
            for e in range(2):
                to_owner(((y + 1) % 4) // 2, e, z_, 1).start()
                to_owner(((y + 3) % 4) // 2, e, z_, 3).start()

    def share(d):
        to_z = (z + d) % 8
        return link(parts.at[to_z], finals.at[d], rz_send.at[d], rz_recv.at[d], device(x, y, to_z, c))

    for d in order:
        z_ = (z + d) % 8

        @pl.when(primary)
        def _():
            three = arrived.at[z_, pl.ds(1, 3)]
            link(three, three, ry_send.at[0, 0], ry_recv.at[z_], other).wait_recv()

        @pl.when(secondary)
        def _():
            link(arrived.at[z_], arrived.at[z_], ry_send.at[0, 0], ry_recv.at[z_], other).wait_recv()

        summed = sum([arrived[z_, k].astype(F32) for k in range(1, 4)], arrived[z_, 0].astype(F32))
        if d:
            parts[z_] = summed.astype(BF16)
            share(d).start()

    for d in range(1, 8):
        share(d).wait_recv()
        summed = summed + finals[d].astype(F32)
    result = summed * (-1.0 / 8.0)
    for k in range(27):
        out_ref[:, 128 * k:128 * k + 128] = result[2 * k:2 * k + 2]

    for d in range(1, 8):
        along_z(d).wait_send()
        share(d).wait_send()
    for n in range(4):
        along_x(n).wait_send()
    for n in range(7):
        across(n).wait_send()
    for n in range(2):
        relay(n).wait_send()
    for d in range(1, 4):
        group(d, 0, 0).wait_send()

    def sent(h, e):
        return link(chunks.at[h, e], chunks.at[h, e], ry_send.at[h, e], ry_recv.at[0], other)

    @pl.when(primary)
    def _():
        sent(mine, 1 - c).wait_send()
        for e in range(2):
            sent(1 - mine, e).wait_send()

    @pl.when(secondary)
    def _():
        group(0, 0, 0).wait_send()
        for h in range(2):
            for e in range(2):
                sent(h, e).wait_send()


def per_device(targets, sources, kpt_coord):
    tables = [jnp.asarray(a) for a in host_tables()]
    vmem = pl.BlockSpec(memory_space=pltpu.VMEM)
    anywhere = pl.BlockSpec(memory_space=pl.ANY)
    sems = pltpu.SemaphoreType.DMA
    out = pl.pallas_call(
        exchange,
        in_specs=[anywhere] * 10,
        out_specs=vmem,
        out_shape=jax.ShapeDtypeStruct((2, 3456), F32),
        scratch_shapes=[
            pltpu.SMEM((3, 8), jnp.int32),
            pltpu.VMEM((2, 3456), BF16),
            pltpu.VMEM((1728, 128), BF16),
        ]
        + [pltpu.VMEM(a.shape, BF16) for a in tables]
        + [
            pltpu.VMEM((64, 128), F32),
            pltpu.VMEM((64, 128), BF16),
            pltpu.VMEM((8, 64, 128), BF16),
            pltpu.VMEM((2, 2, 8, 64, 128), BF16),
            pltpu.VMEM((1744, 128), F32),
            pltpu.VMEM((ROWS, NG * NG), BF16),
            pltpu.VMEM((NG, ROWS, 128), BF16),
            pltpu.VMEM((4, 2, ROWS, NG * NG), BF16),
            pltpu.VMEM((BATCH, NG, ROWS, 128), BF16),
            pltpu.VMEM((BATCH * SPAN, 128), F32),
            pltpu.VMEM((BATCH * SPAN, 128), F32),
            pltpu.VMEM((BATCH, NG, 128), F32),
            pltpu.VMEM((BATCH, NG, 128), F32),
            pltpu.VMEM((NG, ROWS, 128), F32),
            pltpu.VMEM((2, 2, 8, 64, 128), BF16),
            pltpu.VMEM((8, 4, 64, 128), BF16),
            pltpu.VMEM((8, 64, 128), BF16),
            pltpu.VMEM((8, 64, 128), BF16),
            sems((10,)), sems((8,)), sems((8,)), sems((4,)), sems((4, 2)), sems((6,)), sems((6,)),
            sems((7,)), sems((7,)), sems((2, 2)), sems((8,)), sems((8,)), sems((8,)),
        ],
        compiler_params=pltpu.CompilerParams(
            collective_id=0, has_side_effects=True, vmem_limit_bytes=62 * 2**20
        ),
    )(
        kpt_coord.T,
        targets.reshape(2, 3456),
        sources.reshape(2, 864, 128).transpose(1, 0, 2).reshape(1728, 128),
        *tables,
    )
    return out.reshape(1, 1, 2, 3456)


def solution(mesh):
    in_specs = (P("kpt", None, None, "band"), P("kpt", "band", None, None), P())
    out_specs = P("kpt", None, None, "band")
    return jax.shard_map(per_device, mesh=mesh, in_specs=in_specs, out_specs=out_specs, check_vma=False)
```

```python
import functools
import math

import jax
import jax.numpy as jnp
import ml_dtypes
import numpy as np
from jax import lax
from jax.experimental import pallas as pl
from jax.experimental.pallas import tpu as pltpu
from jax.sharding import PartitionSpec as P

NG = 48
ROWS = 2 * NG
PITCH = 104
GROUP1 = 24
GROUP2 = 24
GROUP3 = 24
BATCH = 4
SPAN = NG * PITCH
SPREAD_FROM = (0, 0, 128, 256)
SPREAD_WIDE = (128, 256, 256, 128)
BF16 = jnp.bfloat16
F32 = jnp.float32
MESH = pl.DeviceIdType.MESH


def host_tables():
    index = np.arange(NG)
    phases = ((index[:, None] * index[None, :]) % NG).astype(np.float32) * np.float32(2.0 * math.pi / NG)
    half_type = ml_dtypes.bfloat16
    cosine = np.cos(phases).astype(half_type).astype(np.float32)
    sine = np.sin(phases).astype(half_type).astype(np.float32)
    forward = np.block([[cosine, sine], [-sine, cosine]])
    backward = np.block([[cosine, -sine], [sine, cosine]])

    def lane_table(table):
        wide = np.zeros((2, 2, 64, 2, 2, 64), np.float32)
        for p in range(2):
            for q in range(2):
                for t in range(2):
                    wide[p, t, :NG, q, t, :NG] = table[q * NG:(q + 1) * NG, p * NG:(p + 1) * NG].T
        return wide.reshape(256, 256)

    one = np.zeros((4, 256, 2, 2, 64), np.float32)
    two = np.zeros((4, 512, 2, 2, 64), np.float32)
    gather = np.zeros((3, 4, 2, 64, 128), np.float32)
    for k in range(8):
        lanes = slice(48 * k - SPREAD_FROM[k // 2], 48 * (k + 1) - SPREAD_FROM[k // 2])
        width = SPREAD_WIDE[k // 2]
        for half in range(2):
            one[k // 2, lanes, k % 2, half, :NG] = np.eye(NG)
            two[k // 2, lanes.start + half * width:lanes.stop + half * width, k % 2, half, :NG] = np.eye(NG)
            for chunk in range(3):
                for z in range(NG):
                    lane = 48 * k + z - 128 * chunk
                    if 0 <= lane < 128:
                        gather[chunk, k - 2 * chunk, half, z, lane] = 1
    return [
        a.astype(half_type)
        for a in (
            forward,
            backward,
            lane_table(forward),
            lane_table(backward),
            one.reshape(4, 256, 256),
            two.reshape(4, 512, 256),
            gather.reshape(3, 512, 128),
        )
    ]


def dot(a, b):
    return jnp.dot(a, b, preferred_element_type=F32)


def exchange(
    kpt_hbm, slice_hbm, source_hbm, fwd_hbm, bwd_hbm, zfwd_hbm, zbwd_hbm, one_hbm, two_hbm, gather_hbm, out_ref,
    kpt_ref, slice_ref, raw_ref, fwd_ref, bwd_ref, zfwd_ref, zbwd_ref, one_ref, two_ref, gather_ref,
    staged, piece, carried, slots, rows_f32, dense, targ, sources, src, work1, work2, coul, base, total,
    chunks, arrived, parts, finals,
    in_sem, gz_send, gz_recv, gy_send, gy_recv, s_send, s_recv, c_send, c_recv,
    ry_send, ry_recv, rz_send, rz_recv,
):
    kpt = lax.axis_index("kpt")
    band = lax.axis_index("band")
    x = kpt % 4
    y = (kpt // 4) + ((band // 2) % 2) * 2
    z = band // 4
    c = band % 2
    mine = y // 2
    primary = c == y % 2
    secondary = c != y % 2

    def device(x_, y_, z_, c_):
        return ((y_ % 2) * 4 + x_, z_ * 4 + (y_ // 2) * 2 + c_)

    def link(source, target, send, recv, where):
        return pltpu.make_async_remote_copy(
            src_ref=source, dst_ref=target, send_sem=send, recv_sem=recv, device_id=where, device_id_type=MESH
        )

    x_up = device((x + 1) % 4, y, z, c)
    x_down = device((x + 3) % 4, y, z, c)
    other = device(x, y, z, 1 - c)

    fetched = [
        pltpu.make_async_copy(a, b, in_sem.at[i])
        for i, (a, b) in enumerate(
            (
                (slice_hbm, slice_ref), (source_hbm, raw_ref), (kpt_hbm, kpt_ref), (one_hbm, one_ref),
                (two_hbm, two_ref), (fwd_hbm, fwd_ref), (bwd_hbm, bwd_ref), (zfwd_hbm, zfwd_ref),
                (zbwd_hbm, zbwd_ref), (gather_hbm, gather_ref),
            )
        )
    ]
    for copy in fetched:
        copy.start()

    barrier = pltpu.get_barrier_semaphore()
    peers = [x_up, x_down, other] + [device(x, y, (z + d) % 8, c) for d in range(1, 8)]
    peers += [device(x, (y + d) % 4, z, e) for d in range(1, 4) for e in range(2)]
    for peer in peers:
        pl.semaphore_signal(barrier, inc=1, device_id=peer, device_id_type=MESH)

    fetched[0].wait()
    for k in range(27):
        staged[2 * k:2 * k + 2, :] = slice_ref[:, 128 * k:128 * k + 128].astype(F32)
    piece[...] = staged[...].astype(BF16)

    fetched[1].wait()

    def densify(raw, store):
        for p in range(2):
            for col in range(18):
                store(p, col, raw[pl.ds(2 * col + p, NG, stride=36), :].astype(BF16))

    rows_f32[pl.ds(0, 2 * 864), :] = raw_ref[...].astype(F32)

    def keep_source(p, col, block):
        sources[0, c, p * NG:(p + 1) * NG, col * 128:(col + 1) * 128] = block

    densify(rows_f32, keep_source)

    pl.semaphore_wait(barrier, len(peers))

    def along_z(d):
        return link(piece, carried.at[z], gz_send.at[d], gz_recv.at[d], device(x, y, (z + d) % 8, c))

    def along_y(d, held, z_):
        return link(
            held, slots.at[mine, c, z_], gy_send.at[d], gy_recv.at[d, c], device(x, (y + d) % 4, z, y % 2)
        )

    def spread_y(held, z_):
        for d in range(1, 4):
            along_y(d, held, z_).start()

        @pl.when(secondary)
        def _():
            along_y(0, held, z_).start()

    def outer_first(i):
        return jnp.where(i % 2 == 0, 4 + i // 2, 4 - (i + 1) // 2)

    def repeat(start, stop, act):
        def one(i, carry):
            act(i)
            return carry

        lax.fori_loop(start, stop, one, 0)

    repeat(0, 7, lambda i: along_z(outer_first(i)).start())
    low = pl.ds(0, NG)
    high = pl.ds(NG, NG)
    legs = ((low, 1, x_up), (high, 2, x_down), (high, 1, x_up), (low, 2, x_down))

    def along_x(n):
        part, place, to = legs[n]
        return link(sources.at[0, c, part], sources.at[place, c, part], s_send.at[n], s_recv.at[n], to)

    def relay(n):
        part, place, to = legs[n]
        return link(sources.at[place, c, part], sources.at[3, c, part], s_send.at[4 + n], s_recv.at[4 + n], to)

    def across(n):
        held = sources.at[0, c] if n == 6 else sources.at[(1, 2, 1, 2, 3, 3)[n], c, (low, high)[(0, 1, 1, 0, 0, 1)[n]]]
        return link(held, held, c_send.at[n], c_recv.at[n], other)

    for n in range(4):
        along_x(n).start()
    spread_y(piece, z)
    across(6).start()
    total[...] = jnp.zeros_like(total)

    def forward_slice(i):
        d = jnp.where(i % 2 == 0, 1 + i // 2, 7 - i // 2)
        along_z(d).wait_recv()
        from_z = (z + 8 - d) % 8
        spread_y(carried.at[from_z], from_z)

    repeat(0, 7, forward_slice)

    for n in range(2):
        along_x(n).wait_recv()
        across(n).start()

    for copy in fetched[2:]:
        copy.wait()

    def spread_out(read, table, copies, store):
        for g in range(6):
            for k in range(4):
                width = SPREAD_WIDE[k]
                lanes = slice(384 * g + SPREAD_FROM[k], 384 * g + SPREAD_FROM[k] + width)
                rows = [read(i, lanes) for i in range(copies)]
                wide = dot(rows[0] if copies == 1 else jnp.concatenate(rows, axis=1), table[k, :copies * width, :])
                wide = wide.astype(BF16)
                store(8 * g + 2 * k, wide[:, :128])
                store(8 * g + 2 * k + 1, wide[:, 128:])

    lane = lax.broadcasted_iota(jnp.int32, (NG, 128), 1)
    row = lax.broadcasted_iota(jnp.int32, (NG, 128), 0)

    def frequency(i):
        return jnp.where(i < NG // 2, i, i - NG).astype(F32)

    scale = 4.0 * math.pi / float(NG**3)

    def prepare(num):
        for place, needed in enumerate(((6,), (0, 2), (1, 3), (4, 5))):

            @pl.when(jnp.equal(num, place))
            def _():
                for n in needed:
                    across(n).wait_recv()

        at = num

        def set_source(cell, block):
            src[at, cell] = block

        spread_out(lambda i, lanes: sources[num, i, :, lanes], two_ref, 2, set_source)
        from_x = jnp.where(num == 0, 0, jnp.where(num == 1, 3, jnp.where(num == 2, 1, 2)))
        from_k = (kpt // 4) * 4 + (x + from_x) % 4

        def offset(d):
            return (kpt_ref[d, c * 4 + x] - kpt_ref[d, from_k]).astype(F32) * 0.25

        fx = frequency(row) + offset(0)
        fy = frequency(row) + offset(1)
        fz = frequency(lane % 64) + offset(2)
        coul[at] = 0.04 * (fx * fx)
        base[at] = 0.04 * (fy * fy + fz * fz) + 0.25

    prepare(0)
    forward = fwd_ref[...]
    backward = bwd_ref[...]
    zforward = zfwd_ref[...]
    zbackward = zbwd_ref[...]

    def group(d, h, e):
        whole = slots.at[h, e]
        return link(whole, whole, gy_send.at[d], gy_recv.at[d, e], other)

    for n in range(2, 4):
        along_x(n).wait_recv()
        across(n).start()
    for n in range(2):
        relay(n).start()

    @pl.when(primary)
    def _():
        carried[z] = piece[...]
        slots[mine, c] = carried[...]
        group(0, mine, 1 - c).wait_recv()
        for e in range(2):
            group(2, 1 - mine, e).wait_recv()

    @pl.when(secondary)
    def _():
        for e in range(2):
            group(1, ((y + 3) % 4) // 2, e).wait_recv()
            group(3, ((y + 1) % 4) // 2, e).wait_recv()

    def unpack(z_, carry):
        for h in range(2):
            for e in range(2):
                start = 54 * (4 * z_ + 2 * h + e)
                rows_f32[pl.ds(start, 54), :] = slots[h, e, z_].astype(F32)[:54]
        return carry

    lax.fori_loop(0, 8, unpack, 0)

    def keep_target(p, col, block):
        dense[p * NG:(p + 1) * NG, col * 128:(col + 1) * 128] = block

    densify(rows_f32, keep_target)


    def set_target(cell, block):
        targ[cell] = block

    spread_out(lambda i, lanes: dense[:, lanes], one_ref, 1, set_target)

    def into_spectrum(at, i):
        mixed = []
        for j in range(GROUP1):
            pair = []
            for cell in (2 * (i * GROUP1 + j), 2 * (i * GROUP1 + j) + 1):
                s = src[at, cell].astype(F32)
                t = targ[cell].astype(F32)
                sr, si, tr, ti = s[:NG], s[NG:], t[:NG], t[NG:]
                pair.append(
                    jnp.concatenate([(sr * tr + si * ti).astype(BF16), (sr * ti - si * tr).astype(BF16)], axis=0)
                )
            after_x = dot(forward, jnp.concatenate(pair, axis=1)).astype(BF16)
            for h in (0, 128):
                mixed.append(jnp.concatenate([after_x[:NG, h:h + 128], after_x[NG:, h:h + 128]], axis=1))
        after_z = dot(jnp.concatenate(mixed, axis=0), zforward)
        for j in range(2 * GROUP1):
            for p in range(2):
                start = at * SPAN + (2 * i * GROUP1 + j) * PITCH + p * NG
                work1[pl.ds(start, NG), :] = after_z[j * NG:(j + 1) * NG, p * 128:p * 128 + 128]

    def through_spectrum(at, i):
        for j in range(GROUP2):
            cells = (2 * (i * GROUP2 + j), 2 * (i * GROUP2 + j) + 1)
            pair = [
                jnp.concatenate(
                    [
                        work1[pl.ds(at * SPAN + cell + p * NG, NG, stride=PITCH), :].astype(BF16)
                        for p in range(2)
                    ],
                    axis=0,
                )
                for cell in cells
            ]
            spectrum = dot(forward, jnp.concatenate(pair, axis=1))
            pair = []
            for h, cell in enumerate(cells):
                factor = scale / (base[at] + coul[at, pl.ds(cell, 1), :])
                part = spectrum[:, h * 128:h * 128 + 128]
                pair.append(
                    jnp.concatenate([(part[:NG] * factor).astype(BF16), (part[NG:] * factor).astype(BF16)], axis=0)
                )
            after_y = dot(backward, jnp.concatenate(pair, axis=1))
            for h, cell in enumerate(cells):
                work2[pl.ds(at * SPAN + cell * PITCH, ROWS), :] = after_y[:, h * 128:h * 128 + 128]

    def out_of_spectrum(at, i):
        mixed = [
            jnp.concatenate(
                [
                    work2[pl.ds(at * SPAN + 2 * i * GROUP3 + j + p * NG, NG, stride=PITCH), :].astype(BF16)
                    for p in range(2)
                ],
                axis=1,
            )
            for j in range(2 * GROUP3)
        ]
        after_z = dot(jnp.concatenate(mixed, axis=0), zbackward).astype(BF16)
        for j in range(GROUP3):
            pair = [
                jnp.concatenate([after_z[n * NG:(n + 1) * NG, :128], after_z[n * NG:(n + 1) * NG, 128:]], axis=0)
                for n in (2 * j, 2 * j + 1)
            ]
            potential = dot(backward, jnp.concatenate(pair, axis=1))
            for h in range(2):
                cell = 2 * (i * GROUP3 + j) + h
                s = src[at, cell].astype(F32)
                sr, si = s[:NG], s[NG:]
                pr = potential[:NG, h * 128:h * 128 + 128]
                pi = potential[NG:, h * 128:h * 128 + 128]
                total[cell, :NG, :] += sr * pr - si * pi
                total[cell, NG:, :] += sr * pi + si * pr

    def begin(num, carry):
        @pl.when(num > 0)
        def _():
            prepare(num)

        for i in range(NG // 2 // GROUP1):
            into_spectrum(num, i)
        return carry

    def middle(num, carry):
        @pl.when(num == 2)
        def _():
            for n in range(2):
                relay(n).wait_recv()
                across(4 + n).start()

        for i in range(NG // 2 // GROUP2):
            through_spectrum(num, i)
        return carry

    def finish(num, carry):
        for i in range(NG // 2 // GROUP3):
            out_of_spectrum(num, i)
        return carry

    def stage(num, carry):
        start, stop = 3 * num, 3 + num
        lax.fori_loop(start, stop, begin, 0)
        lax.fori_loop(start, stop, middle, 0)
        return carry

    lax.fori_loop(0, 2, stage, 0)
    lax.fori_loop(0, 4, finish, 0)

    for g in range(6):
        for chunk in range(3):
            cells = [8 * g + 2 * chunk + k for k in range(4)]
            narrow = dot(jnp.concatenate([total[n].astype(BF16) for n in cells], axis=1), gather_ref[chunk])
            for p in range(2):
                rows_f32[pl.ds(2 * (3 * g + chunk) + p, NG, stride=36), :] = narrow[p * NG:(p + 1) * NG]

    def to_owner(h, e, z_, k):
        where = device(x, (y + k) % 4, z, e)
        return link(chunks.at[h, e, z_], arrived.at[z_, k], ry_send.at[h, e], ry_recv.at[z_], where)

    def send_slots(i):
        z_ = (z + outer_first(i)) % 8
        for h in range(2):
            for e in range(2):
                start = 54 * (4 * z_ + 2 * h + e)
                chunks[h, e, z_] = rows_f32[pl.ds(start, 64), :].astype(BF16)

        @pl.when(primary)
        def _():
            to_owner(mine, 1 - c, z_, 0).start()
            for e in range(2):
                to_owner(1 - mine, e, z_, 2).start()
            arrived[z_, 0] = chunks[mine, c, z_]

        @pl.when(secondary)
        def _():
            for e in range(2):
                to_owner(((y + 1) % 4) // 2, e, z_, 1).start()
                to_owner(((y + 3) % 4) // 2, e, z_, 3).start()

    repeat(0, 8, send_slots)

    def share(d):
        to_z = (z + d) % 8
        return link(parts.at[to_z], finals.at[d], rz_send.at[d], rz_recv.at[d], device(x, y, to_z, c))

    def collect(z_):
        @pl.when(primary)
        def _():
            three = arrived.at[z_, pl.ds(1, 3)]
            link(three, three, ry_send.at[0, 0], ry_recv.at[z_], other).wait_recv()

        @pl.when(secondary)
        def _():
            link(arrived.at[z_], arrived.at[z_], ry_send.at[0, 0], ry_recv.at[z_], other).wait_recv()

        return sum([arrived[z_, k].astype(F32) for k in range(1, 4)], arrived[z_, 0].astype(F32))

    def pass_on(i):
        d = outer_first(i)
        z_ = (z + d) % 8
        parts[z_] = collect(z_).astype(BF16)
        share(d).start()

    repeat(0, 7, pass_on)
    summed = collect(z)
    repeat(1, 8, lambda d: share(d).wait_recv())
    summed = sum([finals[d].astype(F32) for d in range(1, 8)], summed)
    result = summed
    for k in range(27):
        out_ref[:, 128 * k:128 * k + 128] = result[2 * k:2 * k + 2]

    def settle(d):
        along_z(d).wait_send()
        share(d).wait_send()

    repeat(1, 8, settle)
    for n in range(4):
        along_x(n).wait_send()
    for n in range(7):
        across(n).wait_send()
    for n in range(2):
        relay(n).wait_send()
    for d in range(1, 4):
        group(d, 0, 0).wait_send()

    def sent(h, e):
        return link(chunks.at[h, e], chunks.at[h, e], ry_send.at[h, e], ry_recv.at[0], other)

    @pl.when(primary)
    def _():
        sent(mine, 1 - c).wait_send()
        for e in range(2):
            sent(1 - mine, e).wait_send()

    @pl.when(secondary)
    def _():
        group(0, 0, 0).wait_send()
        for h in range(2):
            for e in range(2):
                sent(h, e).wait_send()


def per_device(targets, sources, kpt_coord):
    tables = [jnp.asarray(a) for a in host_tables()]
    vmem = pl.BlockSpec(memory_space=pltpu.VMEM)
    anywhere = pl.BlockSpec(memory_space=pl.ANY)
    sems = pltpu.SemaphoreType.DMA
    out = pl.pallas_call(
        exchange,
        in_specs=[anywhere] * 10,
        out_specs=vmem,
        out_shape=jax.ShapeDtypeStruct((2, 3456), F32),
        scratch_shapes=[
            pltpu.SMEM((3, 8), jnp.int32),
            pltpu.VMEM((2, 3456), BF16),
            pltpu.VMEM((1728, 128), BF16),
        ]
        + [pltpu.VMEM(a.shape, BF16) for a in tables]
        + [
            pltpu.VMEM((64, 128), F32),
            pltpu.VMEM((64, 128), BF16),
            pltpu.VMEM((8, 64, 128), BF16),
            pltpu.VMEM((2, 2, 8, 64, 128), BF16),
            pltpu.VMEM((1744, 128), F32),
            pltpu.VMEM((ROWS, NG * NG), BF16),
            pltpu.VMEM((NG, ROWS, 128), BF16),
            pltpu.VMEM((4, 2, ROWS, NG * NG), BF16),
            pltpu.VMEM((BATCH, NG, ROWS, 128), BF16),
            pltpu.VMEM((BATCH * SPAN, 128), F32),
            pltpu.VMEM((BATCH * SPAN, 128), F32),
            pltpu.VMEM((BATCH, NG, 128), F32),
            pltpu.VMEM((BATCH, NG, 128), F32),
            pltpu.VMEM((NG, ROWS, 128), F32),
            pltpu.VMEM((2, 2, 8, 64, 128), BF16),
            pltpu.VMEM((8, 4, 64, 128), BF16),
            pltpu.VMEM((8, 64, 128), BF16),
            pltpu.VMEM((8, 64, 128), BF16),
            sems((10,)), sems((8,)), sems((8,)), sems((4,)), sems((4, 2)), sems((6,)), sems((6,)),
            sems((7,)), sems((7,)), sems((2, 2)), sems((8,)), sems((8,)), sems((8,)),
        ],
        compiler_params=pltpu.CompilerParams(
            collective_id=0, has_side_effects=True, vmem_limit_bytes=62 * 2**20
        ),
    )(
        kpt_coord.T,
        targets.reshape(2, 3456),
        sources.reshape(2, 864, 128).transpose(1, 0, 2).reshape(1728, 128),
        *tables,
    )
    return (out * (-1.0 / 8.0)).reshape(1, 1, 2, 3456)


def solution(mesh):
    in_specs = (P("kpt", None, None, "band"), P("kpt", "band", None, None), P())
    out_specs = P("kpt", None, None, "band")
    return jax.shard_map(per_device, mesh=mesh, in_specs=in_specs, out_specs=out_specs, check_vma=False)
```

```python
import functools
import math

import jax
import jax.numpy as jnp
import ml_dtypes
import numpy as np
from jax import lax
from jax.experimental import pallas as pl
from jax.experimental.pallas import tpu as pltpu
from jax.sharding import PartitionSpec as P

NG = 48
ROWS = 2 * NG
PITCH = 104
GROUP1 = 24
GROUP2 = 24
GROUP3 = 24
BATCH = 4
SPAN = NG * PITCH
SPREAD_FROM = (0, 0, 128, 256)
SPREAD_WIDE = (128, 256, 256, 128)
BF16 = jnp.bfloat16
F32 = jnp.float32
MESH = pl.DeviceIdType.MESH


def host_tables():
    index = np.arange(NG)
    phases = ((index[:, None] * index[None, :]) % NG).astype(np.float32) * np.float32(2.0 * math.pi / NG)
    half_type = ml_dtypes.bfloat16
    cosine = np.cos(phases).astype(half_type).astype(np.float32)
    sine = np.sin(phases).astype(half_type).astype(np.float32)
    forward = np.block([[cosine, sine], [-sine, cosine]])
    backward = np.block([[cosine, -sine], [sine, cosine]])

    def lane_table(table):
        wide = np.zeros((2, 2, 64, 2, 2, 64), np.float32)
        for p in range(2):
            for q in range(2):
                for t in range(2):
                    wide[p, t, :NG, q, t, :NG] = table[q * NG:(q + 1) * NG, p * NG:(p + 1) * NG].T
        return wide.reshape(256, 256)

    one = np.zeros((4, 256, 2, 2, 64), np.float32)
    two = np.zeros((4, 512, 2, 2, 64), np.float32)
    gather = np.zeros((3, 4, 2, 64, 128), np.float32)
    for k in range(8):
        lanes = slice(48 * k - SPREAD_FROM[k // 2], 48 * (k + 1) - SPREAD_FROM[k // 2])
        width = SPREAD_WIDE[k // 2]
        for half in range(2):
            one[k // 2, lanes, k % 2, half, :NG] = np.eye(NG)
            two[k // 2, lanes.start + half * width:lanes.stop + half * width, k % 2, half, :NG] = np.eye(NG)
            for chunk in range(3):
                for z in range(NG):
                    lane = 48 * k + z - 128 * chunk
                    if 0 <= lane < 128:
                        gather[chunk, k - 2 * chunk, half, z, lane] = 1
    return [
        a.astype(half_type)
        for a in (
            forward,
            backward,
            lane_table(forward),
            lane_table(backward),
            one.reshape(4, 256, 256),
            two.reshape(4, 512, 256),
            gather.reshape(3, 512, 128),
        )
    ]


def dot(a, b):
    return jnp.dot(a, b, preferred_element_type=F32)


def exchange(
    kpt_hbm, slice_hbm, source_hbm, fwd_hbm, bwd_hbm, zfwd_hbm, zbwd_hbm, one_hbm, two_hbm, gather_hbm, out_ref,
    kpt_ref, slice_ref, raw_ref, fwd_ref, bwd_ref, zfwd_ref, zbwd_ref, one_ref, two_ref, gather_ref,
    staged, piece, carried, slots, rows_f32, dense, targ, sources, src, work1, work2, coul, base, total,
    chunks, arrived, parts, finals,
    in_sem, gz_send, gz_recv, gy_send, gy_recv, s_send, s_recv, c_send, c_recv,
    ry_send, ry_recv, rz_send, rz_recv,
):
    kpt = lax.axis_index("kpt")
    band = lax.axis_index("band")
    x = kpt % 4
    y = (kpt // 4) + ((band // 2) % 2) * 2
    z = band // 4
    c = band % 2
    mine = y // 2
    primary = c == y % 2
    secondary = c != y % 2

    def device(x_, y_, z_, c_):
        return ((y_ % 2) * 4 + x_, z_ * 4 + (y_ // 2) * 2 + c_)

    def link(source, target, send, recv, where):
        return pltpu.make_async_remote_copy(
            src_ref=source, dst_ref=target, send_sem=send, recv_sem=recv, device_id=where, device_id_type=MESH
        )

    x_up = device((x + 1) % 4, y, z, c)
    x_down = device((x + 3) % 4, y, z, c)
    other = device(x, y, z, 1 - c)

    fetched = [
        pltpu.make_async_copy(a, b, in_sem.at[i])
        for i, (a, b) in enumerate(
            (
                (slice_hbm, slice_ref), (source_hbm, raw_ref), (kpt_hbm, kpt_ref), (one_hbm, one_ref),
                (two_hbm, two_ref), (fwd_hbm, fwd_ref), (bwd_hbm, bwd_ref), (zfwd_hbm, zfwd_ref),
                (zbwd_hbm, zbwd_ref), (gather_hbm, gather_ref),
            )
        )
    ]
    for copy in fetched:
        copy.start()

    barrier = pltpu.get_barrier_semaphore()
    peers = [x_up, x_down, other] + [device(x, y, (z + d) % 8, c) for d in range(1, 8)]
    peers += [device(x, (y + d) % 4, z, e) for d in range(1, 4) for e in range(2)]
    for peer in peers:
        pl.semaphore_signal(barrier, inc=1, device_id=peer, device_id_type=MESH)

    fetched[0].wait()
    for k in range(27):
        staged[2 * k:2 * k + 2, :] = slice_ref[:, 128 * k:128 * k + 128].astype(F32)
    piece[...] = staged[...].astype(BF16)

    fetched[1].wait()

    def densify(raw, store):
        for p in range(2):
            for col in range(18):
                store(p, col, raw[pl.ds(2 * col + p, NG, stride=36), :].astype(BF16))

    rows_f32[pl.ds(0, 2 * 864), :] = raw_ref[...].astype(F32)

    def keep_source(p, col, block):
        sources[0, c, p * NG:(p + 1) * NG, col * 128:(col + 1) * 128] = block

    densify(rows_f32, keep_source)

    pl.semaphore_wait(barrier, len(peers))

    def along_z(d):
        return link(piece, carried.at[z], gz_send.at[d], gz_recv.at[d], device(x, y, (z + d) % 8, c))

    def along_y(d, held, z_):
        return link(
            held, slots.at[mine, c, z_], gy_send.at[d], gy_recv.at[d, c], device(x, (y + d) % 4, z, y % 2)
        )

    def spread_y(held, z_):
        for d in range(1, 4):
            along_y(d, held, z_).start()

        @pl.when(secondary)
        def _():
            along_y(0, held, z_).start()

    def outer_first(i):
        return jnp.where(i % 2 == 0, 4 + i // 2, 4 - (i + 1) // 2)

    def repeat(start, stop, act):
        def one(i, carry):
            act(i)
            return carry

        lax.fori_loop(start, stop, one, 0)

    repeat(0, 7, lambda i: along_z(outer_first(i)).start())
    low = pl.ds(0, NG)
    high = pl.ds(NG, NG)
    legs = ((low, 1, x_up), (high, 2, x_down), (high, 1, x_up), (low, 2, x_down))

    def along_x(n):
        part, place, to = legs[n]
        return link(sources.at[0, c, part], sources.at[place, c, part], s_send.at[n], s_recv.at[n], to)

    def relay(n):
        part, place, to = legs[n]
        return link(sources.at[place, c, part], sources.at[3, c, part], s_send.at[4 + n], s_recv.at[4 + n], to)

    def across(n):
        held = sources.at[0, c] if n == 6 else sources.at[(1, 2, 1, 2, 3, 3)[n], c, (low, high)[(0, 1, 1, 0, 0, 1)[n]]]
        return link(held, held, c_send.at[n], c_recv.at[n], other)

    for n in range(4):
        along_x(n).start()
    spread_y(piece, z)
    across(6).start()
    total[...] = jnp.zeros_like(total)

    def forward_slice(i):
        d = jnp.where(i % 2 == 0, 1 + i // 2, 7 - i // 2)
        along_z(d).wait_recv()
        from_z = (z + 8 - d) % 8
        spread_y(carried.at[from_z], from_z)

    repeat(0, 7, forward_slice)

    for n in range(2):
        along_x(n).wait_recv()
        across(n).start()

    for copy in fetched[2:]:
        copy.wait()

    def spread_out(read, table, copies, store):
        for g in range(6):
            for k in range(4):
                width = SPREAD_WIDE[k]
                lanes = slice(384 * g + SPREAD_FROM[k], 384 * g + SPREAD_FROM[k] + width)
                rows = [read(i, lanes) for i in range(copies)]
                wide = dot(rows[0] if copies == 1 else jnp.concatenate(rows, axis=1), table[k, :copies * width, :])
                wide = wide.astype(BF16)
                store(8 * g + 2 * k, wide[:, :128])
                store(8 * g + 2 * k + 1, wide[:, 128:])

    lane = lax.broadcasted_iota(jnp.int32, (NG, 128), 1)
    row = lax.broadcasted_iota(jnp.int32, (NG, 128), 0)

    def frequency(i):
        return jnp.where(i < NG // 2, i, i - NG).astype(F32)

    scale = 4.0 * math.pi / float(NG**3)

    def prepare(num):
        for place, needed in enumerate(((6,), (0, 2), (1, 3), (4, 5))):

            @pl.when(jnp.equal(num, place))
            def _():
                for n in needed:
                    across(n).wait_recv()

        at = num

        def set_source(cell, block):
            src[at, cell] = block

        spread_out(lambda i, lanes: sources[num, i, :, lanes], two_ref, 2, set_source)
        from_x = jnp.where(num == 0, 0, jnp.where(num == 1, 3, jnp.where(num == 2, 1, 2)))
        from_k = (kpt // 4) * 4 + (x + from_x) % 4

        def offset(d):
            return (kpt_ref[d, c * 4 + x] - kpt_ref[d, from_k]).astype(F32) * 0.25

        fx = frequency(row) + offset(0)
        fy = frequency(row) + offset(1)
        fz = frequency(lane % 64) + offset(2)
        coul[at] = 0.04 * (fx * fx)
        base[at] = 0.04 * (fy * fy + fz * fz) + 0.25

    prepare(0)
    forward = fwd_ref[...]
    backward = bwd_ref[...]
    zforward = zfwd_ref[...]
    zbackward = zbwd_ref[...]

    def group(d, h, e):
        whole = slots.at[h, e]
        return link(whole, whole, gy_send.at[d], gy_recv.at[d, e], other)

    for n in range(2, 4):
        along_x(n).wait_recv()
        across(n).start()
    for n in range(2):
        relay(n).start()

    @pl.when(primary)
    def _():
        carried[z] = piece[...]
        slots[mine, c] = carried[...]
        group(0, mine, 1 - c).wait_recv()
        for e in range(2):
            group(2, 1 - mine, e).wait_recv()

    @pl.when(secondary)
    def _():
        for e in range(2):
            group(1, ((y + 3) % 4) // 2, e).wait_recv()
            group(3, ((y + 1) % 4) // 2, e).wait_recv()

    def unpack(z_, carry):
        for h in range(2):
            for e in range(2):
                start = 54 * (4 * z_ + 2 * h + e)
                rows_f32[pl.ds(start, 54), :] = slots[h, e, z_].astype(F32)[:54]
        return carry

    lax.fori_loop(0, 8, unpack, 0)

    def keep_target(p, col, block):
        dense[p * NG:(p + 1) * NG, col * 128:(col + 1) * 128] = block

    densify(rows_f32, keep_target)


    def set_target(cell, block):
        targ[cell] = block

    spread_out(lambda i, lanes: dense[:, lanes], one_ref, 1, set_target)

    def into_spectrum(at, i):
        mixed = []
        for j in range(GROUP1):
            pair = []
            for cell in (2 * (i * GROUP1 + j), 2 * (i * GROUP1 + j) + 1):
                s = src[at, cell].astype(F32)
                t = targ[cell].astype(F32)
                sr, si, tr, ti = s[:NG], s[NG:], t[:NG], t[NG:]
                pair.append(
                    jnp.concatenate([(sr * tr + si * ti).astype(BF16), (sr * ti - si * tr).astype(BF16)], axis=0)
                )
            after_x = dot(forward, jnp.concatenate(pair, axis=1)).astype(BF16)
            for h in (0, 128):
                mixed.append(jnp.concatenate([after_x[:NG, h:h + 128], after_x[NG:, h:h + 128]], axis=1))
        after_z = dot(jnp.concatenate(mixed, axis=0), zforward)
        for j in range(2 * GROUP1):
            for p in range(2):
                start = at * SPAN + (2 * i * GROUP1 + j) * PITCH + p * NG
                work1[pl.ds(start, NG), :] = after_z[j * NG:(j + 1) * NG, p * 128:p * 128 + 128]

    def through_spectrum(at, i):
        for j in range(GROUP2):
            cells = (2 * (i * GROUP2 + j), 2 * (i * GROUP2 + j) + 1)
            pair = [
                jnp.concatenate(
                    [
                        work1[pl.ds(at * SPAN + cell + p * NG, NG, stride=PITCH), :].astype(BF16)
                        for p in range(2)
                    ],
                    axis=0,
                )
                for cell in cells
            ]
            spectrum = dot(forward, jnp.concatenate(pair, axis=1))
            pair = []
            for h, cell in enumerate(cells):
                factor = scale / (base[at] + coul[at, pl.ds(cell, 1), :])
                part = spectrum[:, h * 128:h * 128 + 128]
                pair.append(
                    jnp.concatenate([(part[:NG] * factor).astype(BF16), (part[NG:] * factor).astype(BF16)], axis=0)
                )
            after_y = dot(backward, jnp.concatenate(pair, axis=1))
            for h, cell in enumerate(cells):
                work2[pl.ds(at * SPAN + cell * PITCH, ROWS), :] = after_y[:, h * 128:h * 128 + 128]

    def out_of_spectrum(at, i):
        mixed = [
            jnp.concatenate(
                [
                    work2[pl.ds(at * SPAN + 2 * i * GROUP3 + j + p * NG, NG, stride=PITCH), :].astype(BF16)
                    for p in range(2)
                ],
                axis=1,
            )
            for j in range(2 * GROUP3)
        ]
        after_z = dot(jnp.concatenate(mixed, axis=0), zbackward).astype(BF16)
        for j in range(GROUP3):
            pair = [
                jnp.concatenate([after_z[n * NG:(n + 1) * NG, :128], after_z[n * NG:(n + 1) * NG, 128:]], axis=0)
                for n in (2 * j, 2 * j + 1)
            ]
            potential = dot(backward, jnp.concatenate(pair, axis=1))
            for h in range(2):
                cell = 2 * (i * GROUP3 + j) + h
                s = src[at, cell].astype(F32)
                sr, si = s[:NG], s[NG:]
                pr = potential[:NG, h * 128:h * 128 + 128]
                pi = potential[NG:, h * 128:h * 128 + 128]
                total[cell, :NG, :] += sr * pr - si * pi
                total[cell, NG:, :] += sr * pi + si * pr

    def begin(num, carry):
        @pl.when(num > 0)
        def _():
            prepare(num)

        for i in range(NG // 2 // GROUP1):
            into_spectrum(num, i)
        return carry

    def middle(num, carry):
        @pl.when(num == 2)
        def _():
            for n in range(2):
                relay(n).wait_recv()
                across(4 + n).start()

        for i in range(NG // 2 // GROUP2):
            through_spectrum(num, i)
        return carry

    def finish(num, carry):
        for i in range(NG // 2 // GROUP3):
            out_of_spectrum(num, i)
        return carry

    def stage(num, carry):
        start, stop = 3 * num, 3 + num
        lax.fori_loop(start, stop, begin, 0)
        lax.fori_loop(start, stop, middle, 0)
        return carry

    lax.fori_loop(0, 2, stage, 0)
    lax.fori_loop(0, 4, finish, 0)

    for g in range(6):
        for chunk in range(3):
            cells = [8 * g + 2 * chunk + k for k in range(4)]
            narrow = dot(jnp.concatenate([total[n].astype(BF16) for n in cells], axis=1), gather_ref[chunk])
            for p in range(2):
                rows_f32[pl.ds(2 * (3 * g + chunk) + p, NG, stride=36), :] = narrow[p * NG:(p + 1) * NG]

    def to_owner(h, e, z_, k):
        where = device(x, (y + k) % 4, z, e)
        return link(chunks.at[h, e, z_], arrived.at[z_, k], ry_send.at[h, e], ry_recv.at[z_], where)

    def send_slots(i):
        z_ = (z + outer_first(i)) % 8
        for h in range(2):
            for e in range(2):
                start = 54 * (4 * z_ + 2 * h + e)
                chunks[h, e, z_] = rows_f32[pl.ds(start, 64), :].astype(BF16)

        @pl.when(primary)
        def _():
            to_owner(mine, 1 - c, z_, 0).start()
            for e in range(2):
                to_owner(1 - mine, e, z_, 2).start()
            arrived[z_, 0] = chunks[mine, c, z_]

        @pl.when(secondary)
        def _():
            for e in range(2):
                to_owner(((y + 1) % 4) // 2, e, z_, 1).start()
                to_owner(((y + 3) % 4) // 2, e, z_, 3).start()

    repeat(0, 8, send_slots)

    def share(d):
        to_z = (z + d) % 8
        return link(parts.at[to_z], finals.at[d], rz_send.at[d], rz_recv.at[d], device(x, y, to_z, c))

    def collect(z_):
        @pl.when(primary)
        def _():
            three = arrived.at[z_, pl.ds(1, 3)]
            link(three, three, ry_send.at[0, 0], ry_recv.at[z_], other).wait_recv()

        @pl.when(secondary)
        def _():
            link(arrived.at[z_], arrived.at[z_], ry_send.at[0, 0], ry_recv.at[z_], other).wait_recv()

        return sum([arrived[z_, k].astype(F32) for k in range(1, 4)], arrived[z_, 0].astype(F32))

    def pass_on(i):
        d = outer_first(i)
        z_ = (z + d) % 8
        parts[z_] = collect(z_).astype(BF16)
        share(d).start()

    repeat(0, 7, pass_on)
    summed = collect(z)
    repeat(1, 8, lambda d: share(d).wait_recv())
    summed = sum([finals[d].astype(F32) for d in range(1, 8)], summed)
    result = summed
    for k in range(27):
        out_ref[:, 128 * k:128 * k + 128] = result[2 * k:2 * k + 2]

    def settle(d):
        along_z(d).wait_send()
        share(d).wait_send()

    repeat(1, 8, settle)
    for n in range(4):
        along_x(n).wait_send()
    for n in range(7):
        across(n).wait_send()
    for n in range(2):
        relay(n).wait_send()
    for d in range(1, 4):
        group(d, 0, 0).wait_send()

    def sent(h, e):
        return link(chunks.at[h, e], chunks.at[h, e], ry_send.at[h, e], ry_recv.at[0], other)

    @pl.when(primary)
    def _():
        sent(mine, 1 - c).wait_send()
        for e in range(2):
            sent(1 - mine, e).wait_send()

    @pl.when(secondary)
    def _():
        group(0, 0, 0).wait_send()
        for h in range(2):
            for e in range(2):
                sent(h, e).wait_send()


def per_device(targets, sources, kpt_coord):
    tables = [jnp.asarray(a) for a in host_tables()]
    vmem = pl.BlockSpec(memory_space=pltpu.VMEM)
    anywhere = pl.BlockSpec(memory_space=pl.ANY)
    sems = pltpu.SemaphoreType.DMA
    out = pl.pallas_call(
        exchange,
        in_specs=[anywhere] * 10,
        out_specs=vmem,
        out_shape=jax.ShapeDtypeStruct((2, 3456), F32),
        scratch_shapes=[
            pltpu.SMEM((3, 8), jnp.int32),
            pltpu.VMEM((2, 3456), BF16),
            pltpu.VMEM((1728, 128), BF16),
        ]
        + [pltpu.VMEM(a.shape, BF16) for a in tables]
        + [
            pltpu.VMEM((64, 128), F32),
            pltpu.VMEM((64, 128), BF16),
            pltpu.VMEM((8, 64, 128), BF16),
            pltpu.VMEM((2, 2, 8, 64, 128), BF16),
            pltpu.VMEM((1792, 128), F32),
            pltpu.VMEM((ROWS, NG * NG), BF16),
            pltpu.VMEM((NG, ROWS, 128), BF16),
            pltpu.VMEM((4, 2, ROWS, NG * NG), BF16),
            pltpu.VMEM((BATCH, NG, ROWS, 128), BF16),
            pltpu.VMEM((BATCH * SPAN + 128, 128), F32),
            pltpu.VMEM((BATCH * SPAN + 128, 128), F32),
            pltpu.VMEM((BATCH, NG, 128), F32),
            pltpu.VMEM((BATCH, NG, 128), F32),
            pltpu.VMEM((NG, ROWS, 128), F32),
            pltpu.VMEM((2, 2, 8, 64, 128), BF16),
            pltpu.VMEM((8, 4, 64, 128), BF16),
            pltpu.VMEM((8, 64, 128), BF16),
            pltpu.VMEM((8, 64, 128), BF16),
            sems((10,)), sems((8,)), sems((8,)), sems((4,)), sems((4, 2)), sems((6,)), sems((6,)),
            sems((7,)), sems((7,)), sems((2, 2)), sems((8,)), sems((8,)), sems((8,)),
        ],
        compiler_params=pltpu.CompilerParams(
            collective_id=0, has_side_effects=True, vmem_limit_bytes=62 * 2**20
        ),
    )(
        kpt_coord.T,
        targets.reshape(2, 3456),
        sources.reshape(2, 864, 128).transpose(1, 0, 2).reshape(1728, 128),
        *tables,
    )
    return (out * (-1.0 / 8.0)).reshape(1, 1, 2, 3456)


def solution(mesh):
    in_specs = (P("kpt", None, None, "band"), P("kpt", "band", None, None), P())
    out_specs = P("kpt", None, None, "band")
    return jax.shard_map(per_device, mesh=mesh, in_specs=in_specs, out_specs=out_specs, check_vma=False)
```

```python
import functools
import math

import jax
import jax.numpy as jnp
import ml_dtypes
import numpy as np
from jax import lax
from jax.experimental import pallas as pl
from jax.experimental.pallas import tpu as pltpu
from jax.sharding import PartitionSpec as P

NG = 48
ROWS = 2 * NG
PITCH = 104
GROUP1 = 24
GROUP2 = 24
GROUP3 = 24
BATCH = 4
SPAN = NG * PITCH
SPREAD_FROM = (0, 0, 128, 256)
SPREAD_WIDE = (128, 256, 256, 128)
BF16 = jnp.bfloat16
F32 = jnp.float32
MESH = pl.DeviceIdType.MESH


def host_tables():
    index = np.arange(NG)
    phases = ((index[:, None] * index[None, :]) % NG).astype(np.float32) * np.float32(2.0 * math.pi / NG)
    half_type = ml_dtypes.bfloat16
    cosine = np.cos(phases).astype(half_type).astype(np.float32)
    sine = np.sin(phases).astype(half_type).astype(np.float32)
    forward = np.block([[cosine, sine], [-sine, cosine]])
    backward = np.block([[cosine, -sine], [sine, cosine]])

    def lane_table(table):
        wide = np.zeros((2, 2, 64, 2, 2, 64), np.float32)
        for p in range(2):
            for q in range(2):
                for t in range(2):
                    wide[p, t, :NG, q, t, :NG] = table[q * NG:(q + 1) * NG, p * NG:(p + 1) * NG].T
        return wide.reshape(256, 256)

    one = np.zeros((4, 256, 2, 2, 64), np.float32)
    two = np.zeros((4, 512, 2, 2, 64), np.float32)
    gather = np.zeros((3, 4, 2, 64, 128), np.float32)
    for k in range(8):
        lanes = slice(48 * k - SPREAD_FROM[k // 2], 48 * (k + 1) - SPREAD_FROM[k // 2])
        width = SPREAD_WIDE[k // 2]
        for half in range(2):
            one[k // 2, lanes, k % 2, half, :NG] = np.eye(NG)
            two[k // 2, lanes.start + half * width:lanes.stop + half * width, k % 2, half, :NG] = np.eye(NG)
            for chunk in range(3):
                for z in range(NG):
                    lane = 48 * k + z - 128 * chunk
                    if 0 <= lane < 128:
                        gather[chunk, k - 2 * chunk, half, z, lane] = 1
    return [
        a.astype(half_type)
        for a in (
            forward,
            backward,
            lane_table(forward),
            lane_table(backward),
            one.reshape(4, 256, 256),
            two.reshape(4, 512, 256),
            gather.reshape(3, 512, 128),
        )
    ]


def dot(a, b):
    return jnp.dot(a, b, preferred_element_type=F32)


def exchange(
    kpt_hbm, slice_hbm, source_hbm, fwd_hbm, bwd_hbm, zfwd_hbm, zbwd_hbm, one_hbm, two_hbm, gather_hbm, out_ref,
    kpt_ref, slice_ref, raw_ref, fwd_ref, bwd_ref, zfwd_ref, zbwd_ref, one_ref, two_ref, gather_ref,
    staged, piece, carried, slots, rows_f32, dense, targ, sources, src, work1, work2, coul, base, total,
    chunks, arrived, parts, finals,
    in_sem, gz_send, gz_recv, gy_send, gy_recv, s_send, s_recv, c_send, c_recv,
    ry_send, ry_recv, rz_send, rz_recv,
):
    kpt = lax.axis_index("kpt")
    band = lax.axis_index("band")
    x = kpt % 4
    y = (kpt // 4) + ((band // 2) % 2) * 2
    z = band // 4
    c = band % 2
    mine = y // 2
    primary = c == y % 2
    secondary = c != y % 2

    def device(x_, y_, z_, c_):
        return ((y_ % 2) * 4 + x_, z_ * 4 + (y_ // 2) * 2 + c_)

    def link(source, target, send, recv, where):
        return pltpu.make_async_remote_copy(
            src_ref=source, dst_ref=target, send_sem=send, recv_sem=recv, device_id=where, device_id_type=MESH
        )

    x_up = device((x + 1) % 4, y, z, c)
    x_down = device((x + 3) % 4, y, z, c)
    other = device(x, y, z, 1 - c)

    fetched = [
        pltpu.make_async_copy(a, b, in_sem.at[i])
        for i, (a, b) in enumerate(
            (
                (slice_hbm, slice_ref), (source_hbm, raw_ref), (kpt_hbm, kpt_ref), (one_hbm, one_ref),
                (two_hbm, two_ref), (fwd_hbm, fwd_ref), (bwd_hbm, bwd_ref), (zfwd_hbm, zfwd_ref),
                (zbwd_hbm, zbwd_ref), (gather_hbm, gather_ref),
            )
        )
    ]
    for copy in fetched:
        copy.start()

    barrier = pltpu.get_barrier_semaphore()
    peers = [x_up, x_down, other] + [device(x, y, (z + d) % 8, c) for d in range(1, 8)]
    peers += [device(x, (y + d) % 4, z, e) for d in range(1, 4) for e in range(2)]
    for peer in peers:
        pl.semaphore_signal(barrier, inc=1, device_id=peer, device_id_type=MESH)

    fetched[0].wait()
    for k in range(27):
        staged[2 * k:2 * k + 2, :] = slice_ref[:, 128 * k:128 * k + 128].astype(F32)
    piece[...] = staged[...].astype(BF16)

    fetched[1].wait()

    def densify(raw, store):
        for p in range(2):
            for col in range(18):
                store(p, col, raw[pl.ds(2 * col + p, NG, stride=36), :].astype(BF16))

    rows_f32[pl.ds(0, 2 * 864), :] = raw_ref[...].astype(F32)

    def keep_source(p, col, block):
        sources[0, c, p * NG:(p + 1) * NG, col * 128:(col + 1) * 128] = block

    densify(rows_f32, keep_source)

    pl.semaphore_wait(barrier, len(peers))

    def along_z(d):
        return link(piece, carried.at[z], gz_send.at[d], gz_recv.at[d], device(x, y, (z + d) % 8, c))

    def along_y(d, held, z_):
        return link(
            held, slots.at[mine, c, z_], gy_send.at[d], gy_recv.at[d, c], device(x, (y + d) % 4, z, y % 2)
        )

    def spread_y(held, z_):
        for d in range(1, 4):
            along_y(d, held, z_).start()

        @pl.when(secondary)
        def _():
            along_y(0, held, z_).start()

    def outer_first(i):
        return jnp.where(i % 2 == 0, 4 + i // 2, 4 - (i + 1) // 2)

    def repeat(start, stop, act):
        def one(i, carry):
            act(i)
            return carry

        lax.fori_loop(start, stop, one, 0)

    low = pl.ds(0, NG)
    high = pl.ds(NG, NG)
    legs = ((low, 1, x_up), (high, 2, x_down), (high, 1, x_up), (low, 2, x_down))

    def along_x(n):
        part, place, to = legs[n]
        return link(sources.at[0, c, part], sources.at[place, c, part], s_send.at[n], s_recv.at[n], to)

    def relay(n):
        part, place, to = legs[n]
        return link(sources.at[place, c, part], sources.at[3, c, part], s_send.at[4 + n], s_recv.at[4 + n], to)

    def across(n):
        held = sources.at[0, c] if n == 6 else sources.at[(1, 2, 1, 2, 3, 3)[n], c, (low, high)[(0, 1, 1, 0, 0, 1)[n]]]
        return link(held, held, c_send.at[n], c_recv.at[n], other)

    for n in range(4):
        along_x(n).start()
    repeat(0, 7, lambda i: along_z(outer_first(i)).start())
    spread_y(piece, z)
    across(6).start()
    total[...] = jnp.zeros_like(total)

    def forward_slice(i):
        d = jnp.where(i % 2 == 0, 1 + i // 2, 7 - i // 2)
        along_z(d).wait_recv()
        from_z = (z + 8 - d) % 8
        spread_y(carried.at[from_z], from_z)

    repeat(0, 7, forward_slice)

    for n in range(2):
        along_x(n).wait_recv()
        across(n).start()

    for copy in fetched[2:]:
        copy.wait()

    def spread_out(read, table, copies, store):
        for g in range(6):
            for k in range(4):
                width = SPREAD_WIDE[k]
                lanes = slice(384 * g + SPREAD_FROM[k], 384 * g + SPREAD_FROM[k] + width)
                rows = [read(i, lanes) for i in range(copies)]
                wide = dot(rows[0] if copies == 1 else jnp.concatenate(rows, axis=1), table[k, :copies * width, :])
                wide = wide.astype(BF16)
                store(8 * g + 2 * k, wide[:, :128])
                store(8 * g + 2 * k + 1, wide[:, 128:])

    lane = lax.broadcasted_iota(jnp.int32, (NG, 128), 1)
    row = lax.broadcasted_iota(jnp.int32, (NG, 128), 0)

    def frequency(i):
        return jnp.where(i < NG // 2, i, i - NG).astype(F32)

    scale = 4.0 * math.pi / float(NG**3)

    def prepare(num):
        for place, needed in enumerate(((6,), (0, 2), (1, 3), (4, 5))):

            @pl.when(jnp.equal(num, place))
            def _():
                for n in needed:
                    across(n).wait_recv()

        at = num

        def set_source(cell, block):
            src[at, cell] = block

        spread_out(lambda i, lanes: sources[num, i, :, lanes], two_ref, 2, set_source)
        from_x = jnp.where(num == 0, 0, jnp.where(num == 1, 3, jnp.where(num == 2, 1, 2)))
        from_k = (kpt // 4) * 4 + (x + from_x) % 4

        def offset(d):
            return (kpt_ref[d, c * 4 + x] - kpt_ref[d, from_k]).astype(F32) * 0.25

        fx = frequency(row) + offset(0)
        fy = frequency(row) + offset(1)
        fz = frequency(lane % 64) + offset(2)
        coul[at] = 0.04 * (fx * fx)
        base[at] = 0.04 * (fy * fy + fz * fz) + 0.25

    prepare(0)
    forward = fwd_ref[...]
    backward = bwd_ref[...]
    zforward = zfwd_ref[...]
    zbackward = zbwd_ref[...]

    def group(d, h, e):
        whole = slots.at[h, e]
        return link(whole, whole, gy_send.at[d], gy_recv.at[d, e], other)

    for n in range(2, 4):
        along_x(n).wait_recv()
        across(n).start()
    for n in range(2):
        relay(n).start()

    @pl.when(primary)
    def _():
        carried[z] = piece[...]
        slots[mine, c] = carried[...]
        group(0, mine, 1 - c).wait_recv()
        for e in range(2):
            group(2, 1 - mine, e).wait_recv()

    @pl.when(secondary)
    def _():
        for e in range(2):
            group(1, ((y + 3) % 4) // 2, e).wait_recv()
            group(3, ((y + 1) % 4) // 2, e).wait_recv()

    def unpack(z_, carry):
        for h in range(2):
            for e in range(2):
                start = 54 * (4 * z_ + 2 * h + e)
                rows_f32[pl.ds(start, 54), :] = slots[h, e, z_].astype(F32)[:54]
        return carry

    lax.fori_loop(0, 8, unpack, 0)

    def keep_target(p, col, block):
        dense[p * NG:(p + 1) * NG, col * 128:(col + 1) * 128] = block

    densify(rows_f32, keep_target)


    def set_target(cell, block):
        targ[cell] = block

    spread_out(lambda i, lanes: dense[:, lanes], one_ref, 1, set_target)

    def into_spectrum(at, i):
        mixed = []
        for j in range(GROUP1):
            pair = []
            for cell in (2 * (i * GROUP1 + j), 2 * (i * GROUP1 + j) + 1):
                s = src[at, cell].astype(F32)
                t = targ[cell].astype(F32)
                sr, si, tr, ti = s[:NG], s[NG:], t[:NG], t[NG:]
                pair.append(
                    jnp.concatenate([(sr * tr + si * ti).astype(BF16), (sr * ti - si * tr).astype(BF16)], axis=0)
                )
            after_x = dot(forward, jnp.concatenate(pair, axis=1)).astype(BF16)
            for h in (0, 128):
                mixed.append(jnp.concatenate([after_x[:NG, h:h + 128], after_x[NG:, h:h + 128]], axis=1))
        after_z = dot(jnp.concatenate(mixed, axis=0), zforward)
        for j in range(2 * GROUP1):
            for p in range(2):
                start = at * SPAN + (2 * i * GROUP1 + j) * PITCH + p * NG
                work1[pl.ds(start, NG), :] = after_z[j * NG:(j + 1) * NG, p * 128:p * 128 + 128]

    def through_spectrum(at, i):
        for j in range(GROUP2):
            cells = (2 * (i * GROUP2 + j), 2 * (i * GROUP2 + j) + 1)
            pair = [
                jnp.concatenate(
                    [
                        work1[pl.ds(at * SPAN + cell + p * NG, NG, stride=PITCH), :].astype(BF16)
                        for p in range(2)
                    ],
                    axis=0,
                )
                for cell in cells
            ]
            spectrum = dot(forward, jnp.concatenate(pair, axis=1))
            pair = []
            for h, cell in enumerate(cells):
                factor = scale / (base[at] + coul[at, pl.ds(cell, 1), :])
                part = spectrum[:, h * 128:h * 128 + 128]
                pair.append(
                    jnp.concatenate([(part[:NG] * factor).astype(BF16), (part[NG:] * factor).astype(BF16)], axis=0)
                )
            after_y = dot(backward, jnp.concatenate(pair, axis=1))
            for h, cell in enumerate(cells):
                work2[pl.ds(at * SPAN + cell * PITCH, ROWS), :] = after_y[:, h * 128:h * 128 + 128]

    def out_of_spectrum(at, i):
        mixed = [
            jnp.concatenate(
                [
                    work2[pl.ds(at * SPAN + 2 * i * GROUP3 + j + p * NG, NG, stride=PITCH), :].astype(BF16)
                    for p in range(2)
                ],
                axis=1,
            )
            for j in range(2 * GROUP3)
        ]
        after_z = dot(jnp.concatenate(mixed, axis=0), zbackward).astype(BF16)
        for j in range(GROUP3):
            pair = [
                jnp.concatenate([after_z[n * NG:(n + 1) * NG, :128], after_z[n * NG:(n + 1) * NG, 128:]], axis=0)
                for n in (2 * j, 2 * j + 1)
            ]
            potential = dot(backward, jnp.concatenate(pair, axis=1))
            for h in range(2):
                cell = 2 * (i * GROUP3 + j) + h
                s = src[at, cell].astype(F32)
                sr, si = s[:NG], s[NG:]
                pr = potential[:NG, h * 128:h * 128 + 128]
                pi = potential[NG:, h * 128:h * 128 + 128]
                total[cell, :NG, :] += sr * pr - si * pi
                total[cell, NG:, :] += sr * pi + si * pr

    def begin(num, carry):
        @pl.when(num > 0)
        def _():
            prepare(num)

        for i in range(NG // 2 // GROUP1):
            into_spectrum(num, i)
        return carry

    def middle(num, carry):
        @pl.when(num == 2)
        def _():
            for n in range(2):
                relay(n).wait_recv()
                across(4 + n).start()

        for i in range(NG // 2 // GROUP2):
            through_spectrum(num, i)
        return carry

    def finish(num, carry):
        for i in range(NG // 2 // GROUP3):
            out_of_spectrum(num, i)
        return carry

    def stage(num, carry):
        start, stop = 3 * num, 3 + num
        lax.fori_loop(start, stop, begin, 0)
        lax.fori_loop(start, stop, middle, 0)
        return carry

    lax.fori_loop(0, 2, stage, 0)
    lax.fori_loop(0, 4, finish, 0)

    for g in range(6):
        for chunk in range(3):
            cells = [8 * g + 2 * chunk + k for k in range(4)]
            narrow = dot(jnp.concatenate([total[n].astype(BF16) for n in cells], axis=1), gather_ref[chunk])
            for p in range(2):
                rows_f32[pl.ds(2 * (3 * g + chunk) + p, NG, stride=36), :] = narrow[p * NG:(p + 1) * NG]

    def to_owner(h, e, z_, k):
        where = device(x, (y + k) % 4, z, e)
        return link(chunks.at[h, e, z_], arrived.at[z_, k], ry_send.at[h, e], ry_recv.at[z_], where)

    def send_slots(i):
        z_ = (z + outer_first(i)) % 8
        for h in range(2):
            for e in range(2):
                start = 54 * (4 * z_ + 2 * h + e)
                chunks[h, e, z_] = rows_f32[pl.ds(start, 64), :].astype(BF16)

        @pl.when(primary)
        def _():
            to_owner(mine, 1 - c, z_, 0).start()
            for e in range(2):
                to_owner(1 - mine, e, z_, 2).start()
            arrived[z_, 0] = chunks[mine, c, z_]

        @pl.when(secondary)
        def _():
            for e in range(2):
                to_owner(((y + 1) % 4) // 2, e, z_, 1).start()
                to_owner(((y + 3) % 4) // 2, e, z_, 3).start()

    repeat(0, 8, send_slots)

    def share(d):
        to_z = (z + d) % 8
        return link(parts.at[to_z], finals.at[d], rz_send.at[d], rz_recv.at[d], device(x, y, to_z, c))

    def collect(z_):
        @pl.when(primary)
        def _():
            three = arrived.at[z_, pl.ds(1, 3)]
            link(three, three, ry_send.at[0, 0], ry_recv.at[z_], other).wait_recv()

        @pl.when(secondary)
        def _():
            link(arrived.at[z_], arrived.at[z_], ry_send.at[0, 0], ry_recv.at[z_], other).wait_recv()

        return sum([arrived[z_, k].astype(F32) for k in range(1, 4)], arrived[z_, 0].astype(F32))

    def pass_on(i):
        d = outer_first(i)
        z_ = (z + d) % 8
        parts[z_] = collect(z_).astype(BF16)
        share(d).start()

    repeat(0, 7, pass_on)
    summed = collect(z)
    repeat(1, 8, lambda d: share(d).wait_recv())
    summed = sum([finals[d].astype(F32) for d in range(1, 8)], summed)
    result = summed
    for k in range(27):
        out_ref[:, 128 * k:128 * k + 128] = result[2 * k:2 * k + 2]

    def settle(d):
        along_z(d).wait_send()
        share(d).wait_send()

    repeat(1, 8, settle)
    for n in range(4):
        along_x(n).wait_send()
    for n in range(7):
        across(n).wait_send()
    for n in range(2):
        relay(n).wait_send()
    for d in range(1, 4):
        group(d, 0, 0).wait_send()

    def sent(h, e):
        return link(chunks.at[h, e], chunks.at[h, e], ry_send.at[h, e], ry_recv.at[0], other)

    @pl.when(primary)
    def _():
        sent(mine, 1 - c).wait_send()
        for e in range(2):
            sent(1 - mine, e).wait_send()

    @pl.when(secondary)
    def _():
        group(0, 0, 0).wait_send()
        for h in range(2):
            for e in range(2):
                sent(h, e).wait_send()


def per_device(targets, sources, kpt_coord):
    tables = [jnp.asarray(a) for a in host_tables()]
    vmem = pl.BlockSpec(memory_space=pltpu.VMEM)
    anywhere = pl.BlockSpec(memory_space=pl.ANY)
    sems = pltpu.SemaphoreType.DMA
    out = pl.pallas_call(
        exchange,
        in_specs=[anywhere] * 10,
        out_specs=vmem,
        out_shape=jax.ShapeDtypeStruct((2, 3456), F32),
        scratch_shapes=[
            pltpu.SMEM((3, 8), jnp.int32),
            pltpu.VMEM((2, 3456), BF16),
            pltpu.VMEM((1728, 128), BF16),
        ]
        + [pltpu.VMEM(a.shape, BF16) for a in tables]
        + [
            pltpu.VMEM((64, 128), F32),
            pltpu.VMEM((64, 128), BF16),
            pltpu.VMEM((8, 64, 128), BF16),
            pltpu.VMEM((2, 2, 8, 64, 128), BF16),
            pltpu.VMEM((1792, 128), F32),
            pltpu.VMEM((ROWS, NG * NG), BF16),
            pltpu.VMEM((NG, ROWS, 128), BF16),
            pltpu.VMEM((4, 2, ROWS, NG * NG), BF16),
            pltpu.VMEM((BATCH, NG, ROWS, 128), BF16),
            pltpu.VMEM((BATCH * SPAN + 128, 128), F32),
            pltpu.VMEM((BATCH * SPAN + 128, 128), F32),
            pltpu.VMEM((BATCH, NG, 128), F32),
            pltpu.VMEM((BATCH, NG, 128), F32),
            pltpu.VMEM((NG, ROWS, 128), F32),
            pltpu.VMEM((2, 2, 8, 64, 128), BF16),
            pltpu.VMEM((8, 4, 64, 128), BF16),
            pltpu.VMEM((8, 64, 128), BF16),
            pltpu.VMEM((8, 64, 128), BF16),
            sems((10,)), sems((8,)), sems((8,)), sems((4,)), sems((4, 2)), sems((6,)), sems((6,)),
            sems((7,)), sems((7,)), sems((2, 2)), sems((8,)), sems((8,)), sems((8,)),
        ],
        compiler_params=pltpu.CompilerParams(
            collective_id=0, has_side_effects=True, vmem_limit_bytes=62 * 2**20
        ),
    )(
        kpt_coord.T,
        targets.reshape(2, 3456),
        sources.reshape(2, 864, 128).transpose(1, 0, 2).reshape(1728, 128),
        *tables,
    )
    return (out * (-1.0 / 8.0)).reshape(1, 1, 2, 3456)


def solution(mesh):
    in_specs = (P("kpt", None, None, "band"), P("kpt", "band", None, None), P())
    out_specs = P("kpt", None, None, "band")
    return jax.shard_map(per_device, mesh=mesh, in_specs=in_specs, out_specs=out_specs, check_vma=False)
```
